256 devices in a mesh: leaf: 128 (over y, x, z), sub: 2 (over core).
Axes of the slice: x: 4, y: 4, z: 8, core: 2. Of those that a mesh axis runs over, the one named last changes fastest.
Arguments:
- rhs: float32 [64, 524288], P(None, ('leaf', 'sub')), may hold values from -6 to 6
- points: float32 [3, 524288], P(None, ('leaf', 'sub')), may hold values from 0 to 1, as said below
- basis: float32 [64, 524288], P(None, ('leaf', 'sub')), may hold values from -0.125 to 0.125
- decay: float32 [64], replicated, may hold values from 0.4 to 0.98
- near_list: int32 [2048, 8], P(('leaf', 'sub')), may hold values from 0 to 2047, as said below
- near_count: int32 [2048], P(('leaf', 'sub')), may hold values from 1 to 8, as said below
Outputs:
- solution: float32 [64, 524288], P(None, ('leaf', 'sub'))
- residual: float32 [64, 524288], P(None, ('leaf', 'sub'))
The draws below stay inside these ranges and needn't reach their ends.
Inputs may be any that keep to these rules, and one draw needn't show every extreme that they name: The points of leaf g lie in the g-th cell of the Morton order of a regular subdivision of the unit cube: bit b of g is bit b // 3 of the cell's index along dimension b % 3. `near_list`: in column k of the list, all leaves of device d name distinct leaves of one device d + s, with s in -1, 0, +1 the same for the whole column and wrapping around the ends of the device order; every leaf is named exactly once in each column. `near_count`: leaf 0 uses all 8 slots.
All inputs are finite; a program needn't handle non-finite values.
Results may differ from the reference program's by a relative error of at most 0.0055.
Values may be sent and summed in bfloat16 or wider, within the bound.
A program may use at most 128 MiB of HBM per device.

```python
import math
import jax
import jax.numpy as jnp
from jax import lax

LEAF = 256
PTS_DEV = 2048
NRHS = 64
RANK = 64
NEAR = 8
ITERS = 3
LEAVES = 8
POINTS = 524288
LEAF_COUNT = 2048
N_LEAF = 128
N_SUB = 2


def draw_points(key, part):
    key = jax.random.fold_in(key, 13)
    nbits = max((LEAF_COUNT - 1).bit_length(), 1)
    leaf_ids = jnp.arange(LEAF_COUNT, dtype=jnp.int32)
    inside = jax.random.uniform(key, (3, LEAF_COUNT, LEAF), jnp.float32, 0.0, 1.0)
    rows = []
    for axis_num in range(3):
        cell_idx = jnp.zeros((LEAF_COUNT,), jnp.int32)
        width_bits = 0
        for bit in range(axis_num, nbits, 3):
            cell_idx = cell_idx + jnp.left_shift(jnp.bitwise_and(jnp.right_shift(leaf_ids, bit), 1), width_bits)
            width_bits = width_bits + 1
        side = 1.0 / float(2 ** width_bits)
        anchor = cell_idx.astype(jnp.float32) * side
        rows.append(anchor[:, None] + side * inside[axis_num])
    return jnp.stack(rows, axis=0).reshape(3, LEAF_COUNT * LEAF).astype(jnp.float32)


def draw_near_list(key, part):
    key = jax.random.fold_in(key, 11)
    ndev = LEAF_COUNT // LEAVES
    key_off, key_perm = jax.random.split(key)
    offset = jax.random.randint(key_off, (), 0, 3)
    steps_dev = (jnp.arange(NEAR, dtype=jnp.int32) + offset) % 3 - 1
    perm_keys = jax.random.split(key_perm, ndev * NEAR)
    perms = jax.vmap(lambda one_key: jax.random.permutation(one_key, LEAVES))(perm_keys)
    perms = perms.reshape(ndev, NEAR, LEAVES).astype(jnp.int32)
    devices = jnp.arange(ndev, dtype=jnp.int32)[:, None, None]
    target = (devices + steps_dev[None, :, None]) % ndev
    global_ids = target * LEAVES + perms
    return global_ids.transpose(0, 2, 1).reshape(LEAF_COUNT, NEAR).astype(jnp.int32)


def draw_near_count(key, part):
    key = jax.random.fold_in(key, 12)
    ndev = LEAF_COUNT // LEAVES
    key_level, key_each = jax.random.split(key)
    level = jax.random.randint(key_level, (ndev, 1), 1, NEAR + 1)
    counts = jax.random.randint(key_each, (ndev, LEAVES), 1, level + 1)
    counts = counts.reshape(LEAF_COUNT).at[0].set(NEAR)
    return counts.astype(jnp.int32)


def block_levels(key, dims, pieces, smallest, top_value):
    loudness = 1.0
    for position, blocks in pieces:
        steps = jax.random.uniform(jax.random.fold_in(jax.random.fold_in(key, 6), position), (blocks,), jnp.float32, smallest / len(pieces), top_value / len(pieces))
        loudness = loudness * jnp.repeat(jnp.exp(steps), dims[position] // blocks).reshape((-1,) + (1,) * (len(dims) - 1 - position))
    return loudness


def bell_draw(stream_key, dims, deviation, limit, cuts=(), kind=jnp.bfloat16):
    result = jax.random.normal(stream_key, dims, jnp.float32) * deviation
    if len(cuts) > 0:
        result = block_levels(stream_key, dims, cuts, -0.22, 0.18) * result
    return jnp.clip(result, min=-limit, max=limit).astype(kind)


def setup_inputs(seed: int = 0) -> dict:
    splits = jax.random.split(jax.random.key(seed), 7)
    return {
        "rhs": bell_draw(splits[0], (NRHS, POINTS), 1.0, 6.0, ((1, 256),), jnp.float32),
        "points": draw_points(jax.random.fold_in(splits[6], 71), 0),
        "basis": bell_draw(splits[2], (RANK, POINTS), PTS_DEV ** -0.5, 0.125, ((1, 256),), jnp.float32),
        "decay": jnp.clip(jnp.exp(jax.random.uniform(splits[3], (RANK,), jnp.float32, math.log(0.4), math.log(0.98))), 0.4, 0.98),
        "near_list": draw_near_list(jax.random.fold_in(splits[6], 71), 0),
        "near_count": draw_near_count(jax.random.fold_in(splits[6], 71), 0),
    }


def kernel(first, second):
    diff = first[..., :, :, None] - second[..., :, None, :]
    dist2 = lax.optimization_barrier(jnp.sum(diff * diff, axis=-3))
    scaled = jnp.sqrt(3.0 * (dist2 + 0.0001)) / 0.08
    return (1.0 + scaled) * jnp.exp(-scaled)

def reference(rhs, points, basis, decay, near_list, near_count):
    ndev = N_LEAF * N_SUB
    coords = points.reshape(3, LEAF_COUNT, LEAF).transpose(1, 0, 2)
    slot_ids = jnp.arange(NEAR, dtype=jnp.int32)
    active = (slot_ids[None, :] < near_count[:, None]).astype(jnp.float32)
    mult = jax.ops.segment_sum(active.reshape(-1), near_list.reshape(-1), num_segments=LEAF_COUNT)
    self_weight = lax.optimization_barrier(jnp.sum(active, axis=1)) + mult
    nbits = (ndev - 1).bit_length()
    dev_ids = jnp.arange(ndev, dtype=jnp.int32)
    differ = jnp.zeros((ndev, ndev), jnp.float32)
    for bit in range(nbits):
        left = jnp.right_shift(dev_ids, bit)
        differ = differ + (left[:, None] != left[None, :]).astype(jnp.float32)
    level_w = jnp.power(decay[None, None, :], differ[:, :, None]) * jnp.power(0.5, (differ[:, :, None] - 1.0) / 2.0)
    level_w = jnp.where((dev_ids[:, None] == dev_ids[None, :])[:, :, None], jnp.ones_like(level_w), level_w)
    basis3 = basis.reshape(RANK, ndev, PTS_DEV)
    hp = lax.Precision.HIGHEST

    def apply(field):
        rounded = field.astype(jnp.bfloat16).reshape(NRHS, LEAF_COUNT, LEAF).transpose(1, 0, 2)

        def self_term(args):
            leaf_pts, leaf_vals = args
            tile = kernel(leaf_pts, leaf_pts).astype(jnp.bfloat16)
            return jnp.einsum('cb,ab->ca', leaf_vals.astype(jnp.float32), tile.astype(jnp.float32))
        totals = lax.map(self_term, (coords, rounded)) * self_weight[:, None, None]
        for slot in range(NEAR):

            def pair_term(args):
                leaf_pts, leaf_vals, other, weight = args
                tile = kernel(leaf_pts, coords[other]).astype(jnp.bfloat16) * weight.astype(jnp.bfloat16)
                tile32 = tile.astype(jnp.float32)
                forward = jnp.einsum('cb,ab->ca', rounded[other].astype(jnp.float32), tile32)
                backward = jnp.einsum('ca,ab->cb', leaf_vals.astype(jnp.float32), tile32)
                return (forward, backward)
            forward, backward = lax.map(pair_term, (coords, rounded, near_list[:, slot], active[:, slot]))
            totals = totals + forward + jax.ops.segment_sum(backward, near_list[:, slot], num_segments=LEAF_COUNT)
        near = totals.transpose(1, 0, 2).reshape(NRHS, POINTS)
        field3 = field.reshape(NRHS, ndev, PTS_DEV)
        coeffs = jnp.einsum('rdq,cdq->drc', basis3, field3, precision=hp)
        mixed = jnp.einsum('der,erc->drc', level_w, coeffs, precision=hp)
        far = jnp.einsum('drc,rdq->cdq', mixed, basis3, precision=hp).reshape(NRHS, POINTS)
        return field + 2.0 / LEAF * near + far
    solution = jnp.zeros_like(rhs)
    residual = rhs
    direction = rhs
    norm_now = lax.optimization_barrier(jnp.sum(residual * residual, axis=1))
    for step in range(ITERS):
        image = apply(direction)
        step_size = norm_now / lax.optimization_barrier(jnp.sum(direction * image, axis=1))
        solution = solution + step_size[:, None] * direction
        residual = residual - step_size[:, None] * image
        norm_next = lax.optimization_barrier(jnp.sum(residual * residual, axis=1))
        direction = residual + (norm_next / norm_now)[:, None] * direction
        norm_now = norm_next
    return (solution, residual)
```

```python
import math
import jax
import jax.numpy as jnp
from jax import lax
from jax.experimental import pallas as pl
from jax.experimental.pallas import tpu as pltpu
from jax.sharding import PartitionSpec as P

LEAF = 256
NEAR = 8
MESH = pl.DeviceIdType.MESH
F32 = jnp.float32
BF16 = jnp.bfloat16
SCALE = math.sqrt(3.0) / 0.08 * math.log2(math.e)
LN2 = math.log(2.0)
RING_HOPS = (0, 1, 2, 1)
Z_MASKS = (8, 10, 6, 12, 14, 4, 2)
XY_MASKS = tuple(
    sorted(range(16, 256, 16), key=lambda m: -(RING_HOPS[(m >> 4) & 3] + RING_HOPS[m >> 6]))
)
N_Z = len(Z_MASKS)
N_XY = len(XY_MASKS)


def level_of(mask):
    return mask.bit_length()


def split2(value):
    high = value.astype(BF16)
    return high, (value - high.astype(F32)).astype(BF16)


def split3(value):
    high = value.astype(BF16).astype(F32)
    rest = value - high
    mid = rest.astype(BF16).astype(F32)
    low = (rest - mid).astype(BF16).astype(F32)
    return high, mid, low


def kernel(
    rhs, pts, basis, dec, lists, x_out, r_out,
    tiles, own_tiles, left_feat, right_feat, stage, gathered, pool0, pool1, pool2, near, basis2, stacked,
    b0, y1, r1, b1, y2, side_pts, side_lists, table_v, table,
    src, sib_in, z_in, xy_in, last_src, last_sib, last_z, last_xy,
    side_ss, side_rs, sib_ss, sib_rs, z_ss, z_rs, xy_ss, xy_rs, table_sem,
):
    nleaf = rhs.shape[1] // LEAF
    pool = (pool0, pool1, pool2)
    me = lax.axis_index("leaf") * 2 + lax.axis_index("sub")
    ndev = 256

    def at(index):
        return (index // 2, lax.rem(index, 2))

    def peer(mask):
        return at(jnp.bitwise_xor(me, mask))

    prev, following = lax.rem(me + ndev - 1, ndev), lax.rem(me + 1, ndev)
    barrier = pltpu.get_barrier_semaphore()
    everyone = [at(prev), at(following), peer(1)] + [peer(m) for m in Z_MASKS + XY_MASKS]
    for other in everyone:
        pl.semaphore_signal(barrier, inc=1, device_id=other, device_id_type=MESH)

    def send(source, target, send_sem, recv_sem, device):
        copy = pltpu.make_async_remote_copy(
            src_ref=source, dst_ref=target, send_sem=send_sem, recv_sem=recv_sem,
            device_id=device, device_id_type=MESH,
        )
        copy.start()
        return copy

    def cols(g):
        return slice(g * LEAF, (g + 1) * LEAF)

    def put_pool(step, g, value):
        pool[step][nleaf + g] = value.astype(BF16)

    def send_sides(step):
        own = pool[step].at[nleaf : 2 * nleaf]
        return [
            send(own, pool[step].at[0:nleaf], side_ss.at[step, 0], side_rs.at[step, 0], at(following)),
            send(own, pool[step].at[2 * nleaf :], side_ss.at[step, 1], side_rs.at[step, 1], at(prev)),
        ]

    lane = lax.broadcasted_iota(jnp.int32, (32, 128), 1)
    low_half = lane < 64
    row16 = lax.broadcasted_iota(jnp.int32, (16, 128), 0)
    row64 = lax.broadcasted_iota(jnp.int32, (64, 128), 0)
    col64 = lax.broadcasted_iota(jnp.int32, (64, 128), 1)

    def to_row(first, second):
        spread = jnp.where(col64 == row64, first, 0.0) + jnp.where(col64 == row64 + 64, second, 0.0)
        return jnp.sum(spread, axis=0, keepdims=True)

    def from_row(row):
        first = jnp.sum(jnp.where(col64 == row64, row, 0.0), axis=1, keepdims=True)
        second = jnp.sum(jnp.where(col64 == row64 + 64, row, 0.0), axis=1, keepdims=True)
        return first, second

    def fold(value):
        return value[:, 0:128] + value[:, 128:256]

    def lanes(value):
        return jnp.sum(value, axis=1, keepdims=True)

    weights = [None, dec[0:1, :]]
    for _ in range(7):
        weights.append(weights[-1] * dec[0:1, :] * math.sqrt(0.5))

    def coeffs(field):
        for g in range(nleaf):
            high, low = split2(field[:, cols(g)])
            stacked[0:64, cols(g)] = high
            stacked[64:128, cols(g)] = low
        full = lax.dot_general(
            stacked[...], basis2[...], (((1,), (1,)), ((), ())), preferred_element_type=F32
        )
        total = full[0:64, 0:128] + full[64:128, 0:128] + full[0:64, 128:256]
        return jnp.where(low_half, total[0:32], total[32:64])

    def write_message(slot, coef, scalars):
        high, mid, low = split3(scalars)
        rows = jnp.where(row16 == 0, high, jnp.where(row16 == 1, mid, jnp.where(row16 == 2, low, 0.0)))
        src[slot, 0:32] = coef.astype(BF16)
        src[slot, 32:48] = rows.astype(BF16)

    def read_message(ref):
        return ref[0:32].astype(F32), jnp.sum(ref[32:48].astype(F32), axis=0, keepdims=True)

    def start_sib(step, coef, scalars):
        write_message(3 * step, coef, scalars)
        return send(src.at[3 * step], sib_in.at[step], sib_ss.at[step], sib_rs.at[step], peer(1))

    def start_z(step, copy, coef, scalars):
        copy.wait()
        other, other_scalars = read_message(sib_in.at[step])
        mixed = coef + weights[1] * other
        total, scalars = coef + other, scalars + other_scalars
        write_message(3 * step + 1, total, scalars)
        copies = [
            send(src.at[3 * step + 1], z_in.at[step, k], z_ss.at[step, k], z_rs.at[step, k], peer(m))
            for k, m in enumerate(Z_MASKS)
        ]
        return copies, mixed, total, scalars

    def collect(copies, masks, buffer, mixed, total, scalars):
        for copy in copies:
            copy.wait()
        levels = {}
        for k, mask in enumerate(masks):
            other, other_scalars = read_message(buffer.at[k])
            level = level_of(mask)
            levels[level] = other if level not in levels else levels[level] + other
            scalars = scalars + other_scalars
        for level, other in levels.items():
            mixed = mixed + weights[level] * other
            total = total + other
        return mixed, total, scalars

    def start_xy(step, copies, mixed, total, scalars):
        mixed, total, scalars = collect(copies, Z_MASKS, z_in.at[step], mixed, total, scalars)
        write_message(3 * step + 2, total, scalars)
        copies = [
            send(src.at[3 * step + 2], xy_in.at[step, k], xy_ss.at[step, k], xy_rs.at[step, k], peer(m))
            for k, m in enumerate(XY_MASKS)
        ]
        return copies, mixed, total, scalars

    def finish(step, copies, mixed, total, scalars):
        mixed, _, scalars = collect(copies, XY_MASKS, xy_in.at[step], mixed, total, scalars)
        both = jnp.concatenate(
            [jnp.where(low_half, mixed, 0.0), jnp.where(low_half, 0.0, mixed)], axis=0
        )
        high, low = split2(both)
        return jnp.concatenate([high, high], axis=1), low, scalars

    def image(g, wide, low):
        far = jnp.dot(wide, basis2[:, cols(g)], preferred_element_type=F32)
        far = far + jnp.dot(low, basis2[0:128, cols(g)], preferred_element_type=F32)
        return near[g] * (2.0 / LEAF) + far

    high, low = split2(basis[...])
    basis2[0:64] = high
    basis2[64:128] = high
    basis2[128:192] = low
    basis2[192:256] = low
    for g in range(nleaf):
        put_pool(0, g, rhs[:, cols(g)])
    coef = coeffs(rhs)
    none = jnp.zeros((1, 128), F32)
    pl.semaphore_wait(barrier, len(everyone))

    side = [
        send(pts, side_pts.at[0], side_ss.at[3, 0], side_rs.at[3, 0], at(following)),
        send(pts, side_pts.at[1], side_ss.at[3, 1], side_rs.at[3, 1], at(prev)),
        send(lists, side_lists.at[0], side_ss.at[4, 0], side_rs.at[4, 0], at(following)),
        send(lists, side_lists.at[1], side_ss.at[4, 1], side_rs.at[4, 1], at(prev)),
    ]
    sib = start_sib(0, coef, none)
    values = send_sides(0)

    center = pts[:, 0:1]
    row8 = lax.broadcasted_iota(jnp.int32, (8, nleaf * LEAF), 0)

    def parts(coords):
        scaled = (coords - center) * SCALE
        norm = jnp.sum(scaled * scaled, axis=0, keepdims=True)
        return split3(scaled), norm

    def left(coords, first):
        (one, two, three), norm = parts(coords)
        n1, n2, n3 = split3(norm + SCALE * SCALE * 0.0001)
        ends = jnp.where(row8 < 6, 1.0, 0.0)
        ends = jnp.where(row8 == 0, n1, jnp.where(row8 == 1, n2, jnp.where(row8 == 2, n3, ends)))
        for k, block in enumerate((one, one, two, two, one, three, ends)):
            stage[8 * k : 8 * k + 8, :] = block
        for g in range(nleaf):
            left_feat[first + g] = jnp.transpose(stage[:, cols(g)]).astype(BF16)

    def right(coords):
        (one, two, three), norm = parts(coords)
        n1, n2, n3 = split3(norm)
        ends = jnp.where(row8 < 3, 1.0, 0.0)
        ends = jnp.where(row8 == 3, n1, jnp.where(row8 == 4, n2, jnp.where(row8 == 5, n3, ends)))
        one, two, three = -2.0 * one, -2.0 * two, -2.0 * three
        for k, block in enumerate((one, two, one, two, three, one, ends)):
            stage[8 * k : 8 * k + 8, :] = block
        for g in range(nleaf):
            right_feat[g] = stage[:, cols(g)].astype(BF16)

    stage[56:, :] = jnp.zeros((stage.shape[0] - 56, nleaf * LEAF), F32)
    right(pts[...])
    left(pts[...], nleaf)

    def tile(leaf, g, one, slope):
        square = jnp.dot(left_feat[leaf], right_feat[g], preferred_element_type=F32)
        root = square * lax.rsqrt(square)
        return (jnp.exp2(-root) * (one + slope * root)).astype(BF16)

    z, mixed, total, scalars = start_z(0, sib, coef, none)

    def self_tile(g, carry):
        own_tiles[g] = tile(nleaf + g, g, 1.0, LN2)
        return carry

    lax.fori_loop(0, nleaf, self_tile, 0)

    for copy in side:
        copy.wait()
    left(side_pts[0], 0)
    left(side_pts[1], 2 * nleaf)

    row = lax.broadcasted_iota(jnp.int32, (8, 128), 0)
    slot = lax.broadcasted_iota(jnp.int32, (8, 128), 1)
    mine = lists[...]
    counts = mine[:, NEAR : NEAR + 1]
    place = jnp.bitwise_and(jnp.right_shift(mine, 3) - me + 1, ndev - 1)
    index = jnp.clip(place * nleaf + jnp.bitwise_and(mine, nleaf - 1), 0, 3 * nleaf - 1)
    table_v[0] = index
    table_v[2] = (slot < counts).astype(jnp.int32)
    named = jnp.zeros((8, 128), jnp.int32)
    named_active = jnp.zeros((8, 128), jnp.int32)
    for k, theirs in enumerate((side_lists[0], mine, side_lists[1])):
        live = (slot < theirs[:, NEAR : NEAR + 1]).astype(jnp.int32)
        for g in range(nleaf):
            match = theirs == me * nleaf + g
            where = jnp.sum(jnp.where(match, row + k * nleaf, 0), axis=0, keepdims=True)
            alive = jnp.sum(jnp.where(match, live, 0), axis=0, keepdims=True)
            named = named + jnp.where(row == g, where, 0)
            named_active = named_active + jnp.where(row == g, alive, 0)
    table_v[1] = jnp.clip(named, 0, 3 * nleaf - 1)
    table_v[3] = named_active
    times = counts + jnp.sum(jnp.where(slot < NEAR, named_active, 0), axis=1, keepdims=True)
    table_v[4] = jnp.broadcast_to(times, (8, 128))
    to_table = pltpu.make_async_copy(table_v, table, table_sem)
    to_table.start()
    to_table.wait()

    def apply_near(step, g):
        for k in range(NEAR):
            gathered[:, k * LEAF : (k + 1) * LEAF] = pool[step][table[0, g, k]]
            gathered[:, (NEAR + k) * LEAF : (NEAR + k + 1) * LEAF] = pool[step][table[1, g, k]]
        others = jnp.dot(gathered[...], tiles[g], preferred_element_type=F32)
        own = jnp.dot(pool[step][nleaf + g], own_tiles[g], preferred_element_type=F32)
        near[g] = others + table[4, g, 0].astype(F32) * own

    for copy in values:
        copy.wait()
    xy, mixed, total, scalars = start_xy(0, z, mixed, total, scalars)

    def first_near(g, carry):
        def half(h, carry):
            for k in range(NEAR):
                one = table[2 + h, g, k].astype(F32)
                value = tile(table[h, g, k], g, one, one * LN2)
                tiles[g, pl.ds(pl.multiple_of((h * NEAR + k) * LEAF, LEAF), LEAF), :] = value
            return carry

        lax.fori_loop(0, 2, half, 0)
        apply_near(0, g)
        return carry

    lax.fori_loop(0, nleaf, first_near, 0)

    def later_near(step, values):
        for copy in values:
            copy.wait()

        def one_leaf(g, carry):
            apply_near(step, g)
            return carry

        lax.fori_loop(0, nleaf, one_leaf, 0)

    wide, low, _ = finish(0, xy, mixed, total, scalars)
    rr = jnp.zeros((64, 128), F32)
    rb = jnp.zeros((64, 128), F32)
    for g in range(nleaf):
        value = image(g, wide, low)
        b0[:, cols(g)] = value
        put_pool(1, g, value)
        held = rhs[:, cols(g)]
        rr = rr + fold(held * held)
        rb = rb + fold(held * value)
    values = send_sides(1)
    scalars = to_row(lanes(rr), lanes(rb))
    coef = coeffs(b0)
    sib = start_sib(1, coef, scalars)
    z, mixed, total, scalars = start_z(1, sib, coef, scalars)
    xy, mixed, total, scalars = start_xy(1, z, mixed, total, scalars)
    later_near(1, values)

    wide, low, scalars = finish(1, xy, mixed, total, scalars)
    rr0, rb0 = from_row(scalars)
    alpha0 = rr0 / (rr0 + rb0)
    rr = jnp.zeros((64, 128), F32)
    rb = jnp.zeros((64, 128), F32)
    for g in range(nleaf):
        value = image(g, wide, low)
        y1[:, cols(g)] = value
        one = b0[:, cols(g)]
        held = rhs[:, cols(g)]
        res = held - alpha0 * (held + one)
        nxt = one - alpha0 * (one + value)
        r1[:, cols(g)] = res
        b1[:, cols(g)] = nxt
        put_pool(2, g, nxt)
        rr = rr + fold(res * res)
        rb = rb + fold(res * nxt)
    values = send_sides(2)
    scalars = to_row(lanes(rr), lanes(rb))
    coef = coeffs(b1)
    sib = start_sib(2, coef, scalars)
    z, mixed, total, scalars = start_z(2, sib, coef, scalars)
    xy, mixed, total, scalars = start_xy(2, z, mixed, total, scalars)
    later_near(2, values)

    wide, low, scalars = finish(2, xy, mixed, total, scalars)
    rr1, rb1 = from_row(scalars)
    beta0 = rr1 / rr0
    alpha1 = rr1 / (rr1 + rb1 - beta0 * rr1 / alpha0)
    rr = jnp.zeros((64, 128), F32)
    rb = jnp.zeros((64, 128), F32)
    for g in range(nleaf):
        value = image(g, wide, low) + beta0 * y1[:, cols(g)]
        direction = r1[:, cols(g)] + beta0 * rhs[:, cols(g)]
        moved = b1[:, cols(g)] + beta0 * b0[:, cols(g)]
        res = r1[:, cols(g)] - alpha1 * (direction + moved)
        nxt = b1[:, cols(g)] - alpha1 * (moved + value)
        y1[:, cols(g)] = direction
        b0[:, cols(g)] = moved
        y2[:, cols(g)] = nxt
        r1[:, cols(g)] = res
        rr = rr + fold(res * res)
        rb = rb + fold(res * nxt)
    scalars = to_row(lanes(rr), lanes(rb))

    last_src[0] = jnp.broadcast_to(scalars, (8, 128))
    copy = send(last_src.at[0], last_sib, sib_ss.at[3], sib_rs.at[3], peer(1))
    copy.wait()
    scalars = scalars + last_sib[0:1]
    for stage_num, (masks, buffer, ss, rs) in enumerate(
        ((Z_MASKS, last_z, z_ss, z_rs), (XY_MASKS, last_xy, xy_ss, xy_rs))
    ):
        last_src[1 + stage_num] = jnp.broadcast_to(scalars, (8, 128))
        copies = [
            send(last_src.at[1 + stage_num], buffer.at[k], ss.at[3, k], rs.at[3, k], peer(m))
            for k, m in enumerate(masks)
        ]
        for copy in copies:
            copy.wait()
        for k in range(len(masks)):
            scalars = scalars + buffer[k, 0:1]
    rr2, rb2 = from_row(scalars)
    beta1 = rr2 / rr1
    alpha2 = rr2 / (rr2 + rb2 - beta1 * rr2 / alpha1)
    for g in range(nleaf):
        direction = r1[:, cols(g)] + beta1 * y1[:, cols(g)]
        moved = y2[:, cols(g)] + beta1 * b0[:, cols(g)]
        r_out[:, cols(g)] = r1[:, cols(g)] - alpha2 * (direction + moved)
        x_out[:, cols(g)] = (
            alpha0 * rhs[:, cols(g)] + alpha1 * y1[:, cols(g)] + alpha2 * direction
        )


def body(rhs, points, basis, decay, near_list, near_count):
    nrows, npts = rhs.shape
    nleaf = npts // LEAF
    pts = jnp.pad(points, ((0, 5), (0, 0)))
    lists = jnp.concatenate([near_list, near_count[:, None]], axis=1)
    lists = jnp.pad(lists, ((0, 0), (0, 128 - NEAR - 1)))
    dec = jnp.broadcast_to(jnp.concatenate([decay, decay])[None, :], (8, 128))
    vmem = pl.BlockSpec(memory_space=pltpu.VMEM)
    field = pltpu.VMEM((nrows, npts), F32)
    dma = pltpu.SemaphoreType.DMA
    shape = jax.ShapeDtypeStruct((nrows, npts), F32)
    return pl.pallas_call(
        kernel,
        out_shape=(shape, shape),
        in_specs=[vmem] * 5,
        out_specs=(vmem, vmem),
        scratch_shapes=[
            pltpu.VMEM((nleaf, 2 * NEAR * LEAF, LEAF), BF16),
            pltpu.VMEM((nleaf, LEAF, LEAF), BF16),
            pltpu.VMEM((3 * nleaf, LEAF, 64), BF16),
            pltpu.VMEM((nleaf, 64, LEAF), BF16),
            pltpu.VMEM((64, npts), F32),
            pltpu.VMEM((nrows, 2 * NEAR * LEAF), BF16),
            *[pltpu.VMEM((3 * nleaf, nrows, LEAF), BF16)] * 3,
            pltpu.VMEM((nleaf, nrows, LEAF), F32),
            pltpu.VMEM((256, npts), BF16),
            pltpu.VMEM((128, npts), BF16),
            field, field, field, field, field,
            pltpu.VMEM((2, 8, npts), F32),
            pltpu.VMEM((2, 8, 128), jnp.int32),
            pltpu.VMEM((5, 8, 128), jnp.int32),
            pltpu.SMEM((5, 8, 128), jnp.int32),
            pltpu.VMEM((9, 48, 128), BF16),
            pltpu.VMEM((3, 48, 128), BF16),
            pltpu.VMEM((3, N_Z, 48, 128), BF16),
            pltpu.VMEM((3, N_XY, 48, 128), BF16),
            pltpu.VMEM((3, 8, 128), F32),
            pltpu.VMEM((8, 128), F32),
            pltpu.VMEM((N_Z, 8, 128), F32),
            pltpu.VMEM((N_XY, 8, 128), F32),
            dma((5, 2)), dma((5, 2)), dma((4,)), dma((4,)),
            dma((4, N_Z)), dma((4, N_Z)), dma((4, N_XY)), dma((4, N_XY)),
            dma,
        ],
        compiler_params=pltpu.CompilerParams(
            collective_id=0, has_side_effects=True, vmem_limit_bytes=56 * 2**20
        ),
    )(rhs, pts, basis, dec, lists)


def solution(mesh):
    in_specs = (
        P(None, ("leaf", "sub")),
        P(None, ("leaf", "sub")),
        P(None, ("leaf", "sub")),
        P(),
        P(("leaf", "sub"), None),
        P(("leaf", "sub")),
    )
    out_specs = (P(None, ("leaf", "sub")), P(None, ("leaf", "sub")))
    return jax.shard_map(body, mesh=mesh, in_specs=in_specs, out_specs=out_specs, check_vma=False)
```

```python
import math
import jax
import jax.numpy as jnp
from jax import lax
from jax.experimental import pallas as pl
from jax.experimental.pallas import tpu as pltpu
from jax.sharding import PartitionSpec as P

LEAF = 256
NEAR = 8
MESH = pl.DeviceIdType.MESH
F32 = jnp.float32
BF16 = jnp.bfloat16
SCALE = math.sqrt(3.0) / 0.08 * math.log2(math.e)
LN2 = math.log(2.0)
RING_HOPS = (0, 1, 2, 1)
Z_MASKS = (8, 10, 6, 12, 14, 4, 2)
XY_MASKS = tuple(
    sorted(range(16, 256, 16), key=lambda m: -(RING_HOPS[(m >> 4) & 3] + RING_HOPS[m >> 6]))
)
N_Z = len(Z_MASKS)
N_XY = len(XY_MASKS)


def level_of(mask):
    return mask.bit_length()


def split2(value):
    high = value.astype(BF16)
    return high, (value - high.astype(F32)).astype(BF16)


def split3(value):
    high = value.astype(BF16).astype(F32)
    rest = value - high
    mid = rest.astype(BF16).astype(F32)
    low = (rest - mid).astype(BF16).astype(F32)
    return high, mid, low


def kernel(
    rhs, pts, basis, decay, near_list, near_count, x_out, r_out,
    tiles, own_tiles, left_feat, right_feat, stage, gathered, pool0, pool1, pool2, near,
    basis2, stacked, gram, b0, y1, r1, b1, r2, b2, lists, side_pts, side_lists, table_v, table,
    part_src0, part_src1, part_in0, part_in1, side_basis, coef_src, coef_in,
    src, sib_in, z_in, xy_in, last_src, last_sib, last_z, last_xy,
    side_ss, side_rs, sib_ss, sib_rs, z_ss, z_rs, xy_ss, xy_rs, part_ss, part_rs,
    basis_ss, basis_rs, coef_ss, coef_rs, table_sem,
):
    nleaf = rhs.shape[1] // LEAF
    pool = (pool0, pool1, pool2)
    part_src = (part_src0, part_src1)
    part_in = (part_in0, part_in1)
    scale = 2.0 / LEAF
    me = lax.axis_index("leaf") * 2 + lax.axis_index("sub")
    ndev = 256

    def at(index):
        return (index // 2, lax.rem(index, 2))

    def peer(mask):
        return at(jnp.bitwise_xor(me, mask))

    prev, following = lax.rem(me + ndev - 1, ndev), lax.rem(me + 1, ndev)
    barrier = pltpu.get_barrier_semaphore()
    everyone = [peer(m) for m in Z_MASKS + XY_MASKS] + [at(prev), at(following), peer(1)]
    for other in everyone:
        pl.semaphore_signal(barrier, inc=1, device_id=other, device_id_type=MESH)

    def send(source, target, send_sem, recv_sem, device):
        copy = pltpu.make_async_remote_copy(
            src_ref=source, dst_ref=target, send_sem=send_sem, recv_sem=recv_sem,
            device_id=device, device_id_type=MESH,
        )
        copy.start()
        return copy

    def cols(g):
        return slice(g * LEAF, (g + 1) * LEAF)

    def put_pool(step, g, value):
        pool[step][nleaf + g] = value.astype(BF16)

    def both_ways(source, targets, send_sems, recv_sems):
        return [
            send(source, targets[0], send_sems[0], recv_sems[0], at(following)),
            send(source, targets[1], send_sems[1], recv_sems[1], at(prev)),
        ]

    def part_copies(step, leaves):
        return [
            pltpu.make_async_remote_copy(
                src_ref=part_src[step].at[leaves], dst_ref=part_in[step].at[side, leaves],
                send_sem=part_ss.at[step, side], recv_sem=part_rs.at[step, side],
                device_id=device, device_id_type=MESH,
            )
            for side, device in enumerate((at(following), at(prev)))
        ]

    def start_part(step, g):
        for copy in part_copies(step, g):
            copy.start()

    def send_coef(step, packed):
        coef_src[step] = packed.astype(BF16)
        return both_ways(
            coef_src.at[step], (coef_in.at[step, 0], coef_in.at[step, 1]),
            (coef_ss.at[step, 0], coef_ss.at[step, 1]), (coef_rs.at[step, 0], coef_rs.at[step, 1]),
        )

    def side_images(step, copies, combine):
        for copy in copies:
            copy.wait()
        for copy in part_copies(step, slice(0, nleaf)):
            copy.wait()
        for side in range(2):
            packed = coef_in[step, side].astype(F32)
            turned = pltpu.roll(packed, 64, 1)
            narrow = jnp.concatenate([packed[:, 0:64], turned[:, 0:64]], axis=0).astype(BF16)
            for g in range(nleaf):
                part = jnp.dot(narrow, side_basis[side, :, cols(g)], preferred_element_type=F32)
                leaf = 2 * nleaf * side + g
                value = part_in[step][side, g].astype(F32) + part
                pool[step + 1][leaf] = combine(leaf, value).astype(BF16)

    lane = lax.broadcasted_iota(jnp.int32, (32, 128), 1)
    low_half = lane < 64
    row16 = lax.broadcasted_iota(jnp.int32, (16, 128), 0)
    row64 = lax.broadcasted_iota(jnp.int32, (64, 128), 0)
    col64 = lax.broadcasted_iota(jnp.int32, (64, 128), 1)

    def to_row(first, second):
        spread = jnp.where(col64 == row64, first, 0.0) + jnp.where(col64 == row64 + 64, second, 0.0)
        return jnp.sum(spread, axis=0, keepdims=True)

    def from_row(row):
        first = jnp.sum(jnp.where(col64 == row64, row, 0.0), axis=1, keepdims=True)
        second = jnp.sum(jnp.where(col64 == row64 + 64, row, 0.0), axis=1, keepdims=True)
        return first, second

    def fold(value):
        return value[:, 0:128] + value[:, 128:256]

    def lanes(value):
        return jnp.sum(value, axis=1, keepdims=True)

    def pack(value):
        value = jnp.broadcast_to(value, (64, 128))
        return jnp.where(low_half, value[0:32], value[32:64])

    def unpack(value):
        return jnp.concatenate(
            [jnp.where(low_half, value, 0.0), jnp.where(low_half, 0.0, value)], axis=0
        )

    decay2 = jnp.concatenate([decay[...], decay[...]], axis=1)
    weights = [None, decay2]
    for _ in range(7):
        weights.append(weights[-1] * decay2 * math.sqrt(0.5))

    def stack(where, value):
        high, low = split2(value)
        stacked[0:64, where] = high
        stacked[64:128, where] = low

    def coeffs():
        full = lax.dot_general(
            stacked[...], basis2[...], (((1,), (1,)), ((), ())), preferred_element_type=F32
        )
        return pack(full[0:64, 0:128] + full[64:128, 0:128] + full[0:64, 128:256])

    def write_message(slot, coef, scalars):
        high, mid, low = split3(scalars)
        rows = jnp.where(row16 == 0, high, jnp.where(row16 == 1, mid, jnp.where(row16 == 2, low, 0.0)))
        src[slot, 0:32] = coef.astype(BF16)
        src[slot, 32:48] = rows.astype(BF16)

    def read_message(ref):
        return ref[0:32].astype(F32), jnp.sum(ref[32:48].astype(F32), axis=0, keepdims=True)

    def start_sib(step, coef, scalars):
        write_message(3 * step, coef, scalars)
        return send(src.at[3 * step], sib_in.at[step], sib_ss.at[step], sib_rs.at[step], peer(1))

    def start_z(step, copy, coef, scalars):
        copy.wait()
        other, other_scalars = read_message(sib_in.at[step])
        mixed = coef + weights[1] * other
        total, scalars = coef + other, scalars + other_scalars
        write_message(3 * step + 1, total, scalars)
        copies = [
            send(src.at[3 * step + 1], z_in.at[step, k], z_ss.at[step, k], z_rs.at[step, k], peer(m))
            for k, m in enumerate(Z_MASKS)
        ]
        return copies, mixed, total, scalars

    def collect(copies, masks, buffer, mixed, total, scalars):
        for copy in copies:
            copy.wait()
        levels = {}
        for k, mask in enumerate(masks):
            other, other_scalars = read_message(buffer.at[k])
            level = level_of(mask)
            levels[level] = other if level not in levels else levels[level] + other
            scalars = scalars + other_scalars
        for level, other in levels.items():
            mixed = mixed + weights[level] * other
            total = total + other
        return mixed, total, scalars

    def start_xy(step, copies, mixed, total, scalars):
        mixed, total, scalars = collect(copies, Z_MASKS, z_in.at[step], mixed, total, scalars)
        write_message(3 * step + 2, total, scalars)
        copies = [
            send(src.at[3 * step + 2], xy_in.at[step, k], xy_ss.at[step, k], xy_rs.at[step, k], peer(m))
            for k, m in enumerate(XY_MASKS)
        ]
        return copies, mixed, total, scalars

    def finish(step, copies, mixed, total, scalars):
        mixed, _, scalars = collect(copies, XY_MASKS, xy_in.at[step], mixed, total, scalars)
        return mixed, scalars

    def widen(both):
        high, low = split2(both)
        return jnp.concatenate([high, high], axis=1), low

    def far(g, wide, low):
        part = jnp.dot(wide, basis2[:, cols(g)], preferred_element_type=F32)
        return part + jnp.dot(low, basis2[0:128, cols(g)], preferred_element_type=F32)

    def through_gram(wide, low):
        part = jnp.dot(wide, gram[...], preferred_element_type=F32)
        return pack(part + jnp.dot(low, gram[0:128], preferred_element_type=F32))

    high, low = split2(basis[...])
    basis2[0:64] = high
    basis2[64:128] = high
    basis2[128:192] = low
    basis2[192:256] = low
    rr = jnp.zeros((64, 128), F32)
    for g in range(nleaf):
        held = rhs[:, cols(g)]
        put_pool(0, g, held)
        stack(cols(g), held)
        rr = rr + fold(held * held)
    rr_local = lanes(rr)
    coef_r0 = coeffs()
    none = jnp.zeros((1, 128), F32)
    full = lax.dot_general(
        basis2[...], basis2[...], (((1,), (1,)), ((), ())), preferred_element_type=F32
    )
    full = full[0:128, 0:128] + full[0:128, 128:256] + full[128:256, 0:128]
    gram[0:128], gram[128:256] = split2(full)
    row8 = lax.broadcasted_iota(jnp.int32, (8, 128), 0)
    slot = lax.broadcasted_iota(jnp.int32, (8, 128), 1)
    lists[...] = jnp.zeros((8, 128), jnp.int32)
    lists[:, 0:NEAR] = near_list[...]
    row_col = lax.broadcasted_iota(jnp.int32, (8, 8), 0) == lax.broadcasted_iota(jnp.int32, (8, 8), 1)
    lists[:, NEAR : NEAR + 1] = jnp.sum(
        jnp.where(row_col, near_count[...], 0), axis=1, keepdims=True
    )

    center = pts[:, 0:1]
    wide8 = lax.broadcasted_iota(jnp.int32, (8, nleaf * LEAF), 0)

    def parts(coords):
        scaled = (coords - center) * SCALE
        norm = jnp.sum(scaled * scaled, axis=0, keepdims=True)
        return split3(scaled), norm

    def left(coords, first):
        (one, two, three), norm = parts(coords)
        n1, n2, n3 = split3(norm + SCALE * SCALE * 0.0001)
        ends = jnp.where(wide8 < 6, 1.0, 0.0)
        ends = jnp.where(wide8 == 0, n1, jnp.where(wide8 == 1, n2, jnp.where(wide8 == 2, n3, ends)))
        for k, block in enumerate((one, one, two, two, one, three)):
            stage[8 * k : 8 * k + 3, :] = block
        stage[48:56, :] = ends
        for g in range(nleaf):
            left_feat[first + g] = jnp.transpose(stage[:, cols(g)]).astype(BF16)

    def right(coords):
        (one, two, three), norm = parts(coords)
        n1, n2, n3 = split3(norm)
        ends = jnp.where(wide8 < 3, 1.0, 0.0)
        ends = jnp.where(wide8 == 3, n1, jnp.where(wide8 == 4, n2, jnp.where(wide8 == 5, n3, ends)))
        one, two, three = -2.0 * one, -2.0 * two, -2.0 * three
        for k, block in enumerate((one, two, one, two, three, one)):
            stage[8 * k : 8 * k + 3, :] = block
        stage[48:56, :] = ends
        for g in range(nleaf):
            right_feat[g] = stage[:, cols(g)].astype(BF16)

    stage[...] = jnp.zeros(stage.shape, F32)
    right(pts[...])
    left(pts[...], nleaf)

    def tile(leaf, g, one, slope):
        square = jnp.dot(left_feat[leaf], right_feat[g], preferred_element_type=F32)
        root = square * lax.rsqrt(square)
        return (jnp.exp2(-root) * (one + slope * root)).astype(BF16)

    for g in range(nleaf):
        own_tiles[g] = tile(nleaf + g, g, 1.0, LN2)
    pl.semaphore_wait(barrier, len(everyone))

    sib = start_sib(0, coef_r0, none)
    side = both_ways(
        pts, (side_pts.at[0], side_pts.at[1]),
        (side_ss.at[0, 0], side_ss.at[0, 1]), (side_rs.at[0, 0], side_rs.at[0, 1]),
    ) + both_ways(
        lists, (side_lists.at[0], side_lists.at[1]),
        (side_ss.at[1, 0], side_ss.at[1, 1]), (side_rs.at[1, 0], side_rs.at[1, 1]),
    )
    z, mixed, total, scalars = start_z(0, sib, coef_r0, none)
    values = both_ways(
        pool0.at[nleaf : 2 * nleaf], (pool0.at[0:nleaf], pool0.at[2 * nleaf :]),
        (side_ss.at[2, 0], side_ss.at[2, 1]), (side_rs.at[2, 0], side_rs.at[2, 1]),
    )
    for copy in side:
        copy.wait()
    left(side_pts[0], 0)
    left(side_pts[1], 2 * nleaf)

    mine = lists[...]
    counts = mine[:, NEAR : NEAR + 1]
    place = jnp.bitwise_and(jnp.right_shift(mine, 3) - me + 1, ndev - 1)
    index = jnp.clip(place * nleaf + jnp.bitwise_and(mine, nleaf - 1), 0, 3 * nleaf - 1)
    table_v[0] = index
    table_v[2] = (slot < counts).astype(jnp.int32)
    named = jnp.zeros((8, 128), jnp.int32)
    named_active = jnp.zeros((8, 128), jnp.int32)
    for k, theirs in enumerate((side_lists[0], mine, side_lists[1])):
        live = (slot < theirs[:, NEAR : NEAR + 1]).astype(jnp.int32)
        for g in range(nleaf):
            match = theirs == me * nleaf + g
            where = jnp.sum(jnp.where(match, row8 + k * nleaf, 0), axis=0, keepdims=True)
            alive = jnp.sum(jnp.where(match, live, 0), axis=0, keepdims=True)
            named = named + jnp.where(row8 == g, where, 0)
            named_active = named_active + jnp.where(row8 == g, alive, 0)
    table_v[1] = jnp.clip(named, 0, 3 * nleaf - 1)
    table_v[3] = named_active
    times = counts + jnp.sum(jnp.where(slot < NEAR, named_active, 0), axis=1, keepdims=True)
    table_v[4] = jnp.broadcast_to(times, (8, 128))
    to_table = pltpu.make_async_copy(table_v, table, table_sem)
    to_table.start()
    to_table.wait()

    def tile_rows(k):
        return slice(k * LEAF, (k + 1) * LEAF)

    def make_tiles(g):
        for h in range(2):
            for k in range(NEAR):
                one = table[2 + h, g, k].astype(F32)
                tiles[2 * g + h, tile_rows(k), :] = tile(table[h, g, k], g, one, one * LN2)

    def near_leaf(step, g):
        for k in range(NEAR):
            gathered[:, tile_rows(k)] = pool[step][table[0, g, k]]
            gathered[:, tile_rows(NEAR + k)] = pool[step][table[1, g, k]]
        total = jnp.dot(pool[step][nleaf + g], own_tiles[g], preferred_element_type=F32)
        total = table[4, g, 0].astype(F32) * total
        for h in range(2):
            total = total + jnp.dot(
                gathered[:, h * NEAR * LEAF : (h + 1) * NEAR * LEAF], tiles[2 * g + h],
                preferred_element_type=F32,
            )
        near[g] = total
        if step < 2:
            part_src[step][g] = (scale * total).astype(BF16)
        stack(pl.ds(pl.multiple_of(g * LEAF, LEAF), LEAF), total)

    def make_both(g, carry):
        near_leaf(0, g - 1)
        make_tiles(g)
        start_part(0, g - 1)
        return carry

    make_tiles(0)
    for copy in values:
        copy.wait()
    bases = both_ways(
        basis2.at[0:64], (side_basis.at[0], side_basis.at[1]),
        (basis_ss.at[0], basis_ss.at[1]), (basis_rs.at[0], basis_rs.at[1]),
    )
    lax.fori_loop(1, 2, make_both, 0)
    xy, mixed, total, scalars = start_xy(0, z, mixed, total, scalars)
    lax.fori_loop(2, nleaf, make_both, 0)
    near_leaf(0, nleaf - 1)
    start_part(0, nleaf - 1)

    def later_near(step):
        def one_leaf(g, carry):
            near_leaf(step, g)
            if step < 2:
                start_part(step, g)
            return carry

        lax.fori_loop(0, nleaf, one_leaf, 0)

    near_coef = coeffs()
    rb = jnp.zeros((64, 128), F32)
    for g in range(nleaf):
        rb = rb + fold(rhs[:, cols(g)] * near[g])
    near_rb = scale * lanes(rb)
    packed, _ = finish(0, xy, mixed, total, scalars)
    side_coefs = send_coef(0, packed)
    both = unpack(packed)
    wide, low = widen(both)
    coef_b0 = scale * near_coef + through_gram(wide, low)
    scalars = to_row(rr_local, near_rb + lanes(unpack(coef_r0) * both))
    coef = coef_b0
    sib = start_sib(1, coef, scalars)
    for g in range(nleaf):
        value = scale * near[g] + far(g, wide, low)
        b0[:, cols(g)] = value
        put_pool(1, g, value)
    z, mixed, total, scalars = start_z(1, sib, coef, scalars)
    for copy in bases:
        copy.wait()
    side_images(0, side_coefs, lambda leaf, value: value)
    xy, mixed, total, scalars = start_xy(1, z, mixed, total, scalars)
    later_near(1)
    near_coef = coeffs()

    packed, scalars = finish(1, xy, mixed, total, scalars)
    side_coefs = send_coef(1, packed)
    both = unpack(packed)
    wide, low = widen(both)
    rr0, rb0 = from_row(scalars)
    alpha0 = rr0 / (rr0 + rb0)
    coef_y1 = scale * near_coef + through_gram(wide, low)
    coef_r1 = coef_r0 - pack(alpha0) * (coef_r0 + coef_b0)
    coef_b1 = coef_b0 - pack(alpha0) * (coef_b0 + coef_y1)
    rr = jnp.zeros((64, 128), F32)
    rb = jnp.zeros((64, 128), F32)
    for g in range(nleaf):
        one = b0[:, cols(g)]
        held = rhs[:, cols(g)]
        res = held - alpha0 * (held + one)
        r1[:, cols(g)] = res
        nxt = one - alpha0 * (one + scale * near[g])
        b1[:, cols(g)] = nxt
        rr = rr + fold(res * res)
        rb = rb + fold(res * nxt)
    scalars = to_row(lanes(rr), lanes(rb) - alpha0 * lanes(unpack(coef_r1) * both))
    coef = coef_b1
    sib = start_sib(2, coef, scalars)
    for g in range(nleaf):
        part = far(g, wide, low)
        y1[:, cols(g)] = scale * near[g] + part
        nxt = b1[:, cols(g)] - alpha0 * part
        b1[:, cols(g)] = nxt
        put_pool(2, g, nxt)
    z, mixed, total, scalars = start_z(2, sib, coef, scalars)
    side_images(
        1, side_coefs,
        lambda leaf, value: pool1[leaf].astype(F32) * (1.0 - alpha0) - alpha0 * value,
    )
    xy, mixed, total, scalars = start_xy(2, z, mixed, total, scalars)
    later_near(2)

    packed, scalars = finish(2, xy, mixed, total, scalars)
    both = unpack(packed)
    wide, low = widen(both)
    rr1, rb1 = from_row(scalars)
    beta0 = rr1 / rr0
    alpha1 = rr1 / (rr1 + rb1 - beta0 * rr1 / alpha0)
    coef_p1 = coef_r1 + pack(beta0) * coef_r0
    coef_r2 = coef_r1 - pack(alpha1) * (coef_p1 + coef_b1 + pack(beta0) * coef_b0)
    rr = jnp.zeros((64, 128), F32)
    rb = jnp.zeros((64, 128), F32)
    for g in range(nleaf):
        direction = r1[:, cols(g)] + beta0 * rhs[:, cols(g)]
        moved = b1[:, cols(g)] + beta0 * b0[:, cols(g)]
        res = r1[:, cols(g)] - alpha1 * (direction + moved)
        nxt = b1[:, cols(g)] - alpha1 * (moved + scale * near[g] + beta0 * y1[:, cols(g)])
        r2[:, cols(g)] = res
        b2[:, cols(g)] = nxt
        rr = rr + fold(res * res)
        rb = rb + fold(res * nxt)
    scalars = to_row(lanes(rr), lanes(rb) - alpha1 * lanes(unpack(coef_r2) * both))

    last_src[0] = jnp.broadcast_to(scalars, (8, 128))
    copy = send(last_src.at[0], last_sib, sib_ss.at[3], sib_rs.at[3], peer(1))
    copy.wait()
    scalars = scalars + last_sib[0:1]
    for stage_num, (masks, buffer, ss, rs) in enumerate(
        ((Z_MASKS, last_z, z_ss, z_rs), (XY_MASKS, last_xy, xy_ss, xy_rs))
    ):
        last_src[1 + stage_num] = jnp.broadcast_to(scalars, (8, 128))
        copies = [
            send(last_src.at[1 + stage_num], buffer.at[k], ss.at[3, k], rs.at[3, k], peer(m))
            for k, m in enumerate(masks)
        ]
        if stage_num == 0:
            for g in range(nleaf):
                direction = r1[:, cols(g)] + beta0 * rhs[:, cols(g)]
                moved = b1[:, cols(g)] + beta0 * b0[:, cols(g)]
                b2[:, cols(g)] = b2[:, cols(g)] - alpha1 * far(g, wide, low)
                y1[:, cols(g)] = direction
                b0[:, cols(g)] = moved
                r1[:, cols(g)] = alpha0 * rhs[:, cols(g)] + alpha1 * direction
        for copy in copies:
            copy.wait()
        for k in range(len(masks)):
            scalars = scalars + buffer[k, 0:1]
    rr2, rb2 = from_row(scalars)
    beta1 = rr2 / rr1
    alpha2 = rr2 / (rr2 + rb2 - beta1 * rr2 / alpha1)
    for g in range(nleaf):
        direction = r2[:, cols(g)] + beta1 * y1[:, cols(g)]
        moved = b2[:, cols(g)] + beta1 * b0[:, cols(g)]
        r_out[:, cols(g)] = r2[:, cols(g)] - alpha2 * (direction + moved)
        x_out[:, cols(g)] = r1[:, cols(g)] + alpha2 * direction


def body(rhs, points, basis, decay, near_list, near_count):
    nrows, npts = rhs.shape
    nleaf = npts // LEAF
    vmem = pl.BlockSpec(memory_space=pltpu.VMEM)
    field = pltpu.VMEM((nrows, npts), F32)
    dma = pltpu.SemaphoreType.DMA
    shape = jax.ShapeDtypeStruct((nrows, npts), F32)
    return pl.pallas_call(
        kernel,
        out_shape=(shape, shape),
        in_specs=[vmem] * 6,
        out_specs=(vmem, vmem),
        scratch_shapes=[
            pltpu.VMEM((2 * nleaf, NEAR * LEAF, LEAF), BF16),
            pltpu.VMEM((nleaf, LEAF, LEAF), BF16),
            pltpu.VMEM((3 * nleaf, LEAF, 64), BF16),
            pltpu.VMEM((nleaf, 64, LEAF), BF16),
            pltpu.VMEM((64, npts), F32),
            pltpu.VMEM((nrows, 2 * NEAR * LEAF), BF16),
            *[pltpu.VMEM((3 * nleaf, nrows, LEAF), BF16)] * 3,
            pltpu.VMEM((nleaf, nrows, LEAF), F32),
            pltpu.VMEM((256, npts), BF16),
            pltpu.VMEM((128, npts), BF16),
            pltpu.VMEM((256, 128), BF16),
            field, field, field, field, field, field,
            pltpu.VMEM((8, 128), jnp.int32),
            pltpu.VMEM((2, 3, npts), F32),
            pltpu.VMEM((2, 8, 128), jnp.int32),
            pltpu.VMEM((5, 8, 128), jnp.int32),
            pltpu.SMEM((5, 8, 128), jnp.int32),
            *[pltpu.VMEM((nleaf, nrows, LEAF), BF16)] * 2,
            *[pltpu.VMEM((2, nleaf, nrows, LEAF), BF16)] * 2,
            pltpu.VMEM((2, 64, npts), BF16),
            pltpu.VMEM((2, 32, 128), BF16),
            pltpu.VMEM((2, 2, 32, 128), BF16),
            pltpu.VMEM((9, 48, 128), BF16),
            pltpu.VMEM((3, 48, 128), BF16),
            pltpu.VMEM((3, N_Z, 48, 128), BF16),
            pltpu.VMEM((3, N_XY, 48, 128), BF16),
            pltpu.VMEM((3, 8, 128), F32),
            pltpu.VMEM((8, 128), F32),
            pltpu.VMEM((N_Z, 8, 128), F32),
            pltpu.VMEM((N_XY, 8, 128), F32),
            dma((3, 2)), dma((3, 2)), dma((4,)), dma((4,)),
            dma((4, N_Z)), dma((4, N_Z)), dma((4, N_XY)), dma((4, N_XY)),
            dma((2, 2)), dma((2, 2)),
            dma((2,)), dma((2,)), dma((2, 2)), dma((2, 2)),
            dma,
        ],
        compiler_params=pltpu.CompilerParams(
            collective_id=0, has_side_effects=True, vmem_limit_bytes=56 * 2**20
        ),
    )(rhs, points, basis, decay[None, :], near_list, near_count[None, :])


def solution(mesh):
    in_specs = (
        P(None, ("leaf", "sub")),
        P(None, ("leaf", "sub")),
        P(None, ("leaf", "sub")),
        P(),
        P(("leaf", "sub"), None),
        P(("leaf", "sub")),
    )
    out_specs = (P(None, ("leaf", "sub")), P(None, ("leaf", "sub")))
    return jax.shard_map(body, mesh=mesh, in_specs=in_specs, out_specs=out_specs, check_vma=False)
```

```python
import math
import jax
import jax.numpy as jnp
from jax import lax
from jax.experimental import pallas as pl
from jax.experimental.pallas import tpu as pltpu
from jax.sharding import PartitionSpec as P

LEAF = 256
NEAR = 8
MESH = pl.DeviceIdType.MESH
F32 = jnp.float32
BF16 = jnp.bfloat16
SCALE = math.sqrt(3.0) / 0.08 * math.log2(math.e)
LN2 = math.log(2.0)
RING_HOPS = (0, 1, 2, 1)
Z_MASKS = (8, 10, 6, 12, 14, 4, 2)
XY_MASKS = tuple(
    sorted(range(16, 256, 16), key=lambda m: -(RING_HOPS[(m >> 4) & 3] + RING_HOPS[m >> 6]))
)
N_Z = len(Z_MASKS)
N_XY = len(XY_MASKS)


def level_of(mask):
    return mask.bit_length()


def split2(value):
    high = value.astype(BF16)
    return high, (value - high.astype(F32)).astype(BF16)


def split3(value):
    high = value.astype(BF16).astype(F32)
    rest = value - high
    mid = rest.astype(BF16).astype(F32)
    low = (rest - mid).astype(BF16).astype(F32)
    return high, mid, low


def kernel(
    rhs, pts, basis, decay, near_list, near_count, x_out, r_out,
    tiles, own_tiles, left_feat, right_feat, stage, gathered, pool0, pool1, pool2, near,
    basis2, stacked, gram, b0, y1, r1, b1, r2, b2, lists, side_pts, side_lists, table_v, table,
    part_src0, part_src1, part_in0, part_in1, side_basis, coef_src, coef_in,
    src, sib_in, z_in, xy_in, last_src, last_sib, last_z, last_xy,
    side_ss, side_rs, sib_ss, sib_rs, z_ss, z_rs, xy_ss, xy_rs, part_ss, part_rs,
    basis_ss, basis_rs, coef_ss, coef_rs, table_sem,
):
    nleaf = rhs.shape[1] // LEAF
    pool = (pool0, pool1, pool2)
    part_src = (part_src0, part_src1)
    part_in = (part_in0, part_in1)
    scale = 2.0 / LEAF
    me = lax.axis_index("leaf") * 2 + lax.axis_index("sub")
    ndev = 256

    def at(index):
        return (index // 2, lax.rem(index, 2))

    def peer(mask):
        return at(jnp.bitwise_xor(me, mask))

    prev, following = lax.rem(me + ndev - 1, ndev), lax.rem(me + 1, ndev)
    barrier = pltpu.get_barrier_semaphore()
    everyone = [peer(m) for m in Z_MASKS + XY_MASKS] + [at(prev), at(following), peer(1)]
    for other in everyone:
        pl.semaphore_signal(barrier, inc=1, device_id=other, device_id_type=MESH)

    def send(source, target, send_sem, recv_sem, device):
        copy = pltpu.make_async_remote_copy(
            src_ref=source, dst_ref=target, send_sem=send_sem, recv_sem=recv_sem,
            device_id=device, device_id_type=MESH,
        )
        copy.start()
        return copy

    def cols(g):
        return slice(g * LEAF, (g + 1) * LEAF)

    def put_pool(step, g, value):
        pool[step][nleaf + g] = value.astype(BF16)

    def both_ways(source, targets, send_sems, recv_sems):
        return [
            send(source, targets[0], send_sems[0], recv_sems[0], at(following)),
            send(source, targets[1], send_sems[1], recv_sems[1], at(prev)),
        ]

    def part_copies(step, leaves):
        return [
            pltpu.make_async_remote_copy(
                src_ref=part_src[step].at[leaves], dst_ref=part_in[step].at[side, leaves],
                send_sem=part_ss.at[step, side], recv_sem=part_rs.at[step, side],
                device_id=device, device_id_type=MESH,
            )
            for side, device in enumerate((at(following), at(prev)))
        ]

    def start_part(step, g):
        for copy in part_copies(step, g):
            copy.start()

    def send_coef(step, packed):
        coef_src[step] = packed.astype(BF16)
        return both_ways(
            coef_src.at[step], (coef_in.at[step, 0], coef_in.at[step, 1]),
            (coef_ss.at[step, 0], coef_ss.at[step, 1]), (coef_rs.at[step, 0], coef_rs.at[step, 1]),
        )

    def side_images(step, copies, combine):
        for copy in copies:
            copy.wait()
        for copy in part_copies(step, slice(0, nleaf)):
            copy.wait()
        for side in range(2):
            packed = coef_in[step, side].astype(F32)
            turned = pltpu.roll(packed, 64, 1)
            narrow = jnp.concatenate([packed[:, 0:64], turned[:, 0:64]], axis=0).astype(BF16)
            for g in range(nleaf):
                part = jnp.dot(narrow, side_basis[side, :, cols(g)], preferred_element_type=F32)
                leaf = 2 * nleaf * side + g
                value = part_in[step][side, g].astype(F32) + part
                pool[step + 1][leaf] = combine(leaf, value).astype(BF16)

    lane = lax.broadcasted_iota(jnp.int32, (32, 128), 1)
    low_half = lane < 64
    row16 = lax.broadcasted_iota(jnp.int32, (16, 128), 0)
    row64 = lax.broadcasted_iota(jnp.int32, (64, 128), 0)
    col64 = lax.broadcasted_iota(jnp.int32, (64, 128), 1)

    def to_row(first, second):
        spread = jnp.where(col64 == row64, first, 0.0) + jnp.where(col64 == row64 + 64, second, 0.0)
        return jnp.sum(spread, axis=0, keepdims=True)

    def from_row(row):
        first = jnp.sum(jnp.where(col64 == row64, row, 0.0), axis=1, keepdims=True)
        second = jnp.sum(jnp.where(col64 == row64 + 64, row, 0.0), axis=1, keepdims=True)
        return first, second

    def fold(value):
        return value[:, 0:128] + value[:, 128:256]

    def lanes(value):
        return jnp.sum(value, axis=1, keepdims=True)

    def pack(value):
        value = jnp.broadcast_to(value, (64, 128))
        return jnp.where(low_half, value[0:32], value[32:64])

    def unpack(value):
        return jnp.concatenate(
            [jnp.where(low_half, value, 0.0), jnp.where(low_half, 0.0, value)], axis=0
        )

    decay2 = jnp.concatenate([decay[...], decay[...]], axis=1)
    weights = [None, decay2]
    for _ in range(7):
        weights.append(weights[-1] * decay2 * math.sqrt(0.5))

    def stack(where, value):
        high, low = split2(value)
        stacked[0:64, where] = high
        stacked[64:128, where] = low

    def coeffs():
        full = lax.dot_general(
            stacked[...], basis2[...], (((1,), (1,)), ((), ())), preferred_element_type=F32
        )
        return pack(full[0:64, 0:128] + full[64:128, 0:128] + full[0:64, 128:256])

    def write_message(slot, coef, scalars):
        high, mid, low = split3(scalars)
        rows = jnp.where(row16 == 0, high, jnp.where(row16 == 1, mid, jnp.where(row16 == 2, low, 0.0)))
        src[slot, 0:32] = coef.astype(BF16)
        src[slot, 32:48] = rows.astype(BF16)

    def read_message(ref):
        return ref[0:32].astype(F32), jnp.sum(ref[32:48].astype(F32), axis=0, keepdims=True)

    def start_sib(step, coef, scalars):
        write_message(3 * step, coef, scalars)
        return send(src.at[3 * step], sib_in.at[step], sib_ss.at[step], sib_rs.at[step], peer(1))

    def start_z(step, copy, coef, scalars):
        copy.wait()
        other, other_scalars = read_message(sib_in.at[step])
        mixed = coef + weights[1] * other
        total, scalars = coef + other, scalars + other_scalars
        write_message(3 * step + 1, total, scalars)
        copies = [
            send(src.at[3 * step + 1], z_in.at[step, k], z_ss.at[step, k], z_rs.at[step, k], peer(m))
            for k, m in enumerate(Z_MASKS)
        ]
        return copies, mixed, total, scalars

    def collect(copies, masks, buffer, mixed, total, scalars):
        for copy in copies:
            copy.wait()
        levels = {}
        for k, mask in enumerate(masks):
            other, other_scalars = read_message(buffer.at[k])
            level = level_of(mask)
            levels[level] = other if level not in levels else levels[level] + other
            scalars = scalars + other_scalars
        for level, other in levels.items():
            mixed = mixed + weights[level] * other
            total = total + other
        return mixed, total, scalars

    def start_xy(step, copies, mixed, total, scalars):
        mixed, total, scalars = collect(copies, Z_MASKS, z_in.at[step], mixed, total, scalars)
        write_message(3 * step + 2, total, scalars)
        copies = [
            send(src.at[3 * step + 2], xy_in.at[step, k], xy_ss.at[step, k], xy_rs.at[step, k], peer(m))
            for k, m in enumerate(XY_MASKS)
        ]
        return copies, mixed, total, scalars

    def finish(step, copies, mixed, total, scalars):
        mixed, _, scalars = collect(copies, XY_MASKS, xy_in.at[step], mixed, total, scalars)
        return mixed, scalars

    def widen(both):
        high, low = split2(both)
        return jnp.concatenate([high, high], axis=1), low

    def far(g, wide, low):
        part = jnp.dot(wide, basis2[:, cols(g)], preferred_element_type=F32)
        return part + jnp.dot(low, basis2[0:128, cols(g)], preferred_element_type=F32)

    def through_gram(wide, low):
        part = jnp.dot(wide, gram[...], preferred_element_type=F32)
        return pack(part + jnp.dot(low, gram[0:128], preferred_element_type=F32))

    high, low = split2(basis[...])
    basis2[0:64] = high
    basis2[64:128] = high
    basis2[128:192] = low
    basis2[192:256] = low
    rr = jnp.zeros((64, 128), F32)
    for g in range(nleaf):
        held = rhs[:, cols(g)]
        put_pool(0, g, held)
        stack(cols(g), held)
        rr = rr + fold(held * held)
    rr_local = lanes(rr)
    coef_r0 = coeffs()
    none = jnp.zeros((1, 128), F32)
    full = lax.dot_general(
        basis2[...], basis2[...], (((1,), (1,)), ((), ())), preferred_element_type=F32
    )
    full = full[0:128, 0:128] + full[0:128, 128:256] + full[128:256, 0:128]
    gram[0:128], gram[128:256] = split2(full)
    row8 = lax.broadcasted_iota(jnp.int32, (8, 128), 0)
    slot = lax.broadcasted_iota(jnp.int32, (8, 128), 1)
    lists[...] = jnp.zeros((8, 128), jnp.int32)
    lists[:, 0:NEAR] = near_list[...]
    row_col = lax.broadcasted_iota(jnp.int32, (8, 8), 0) == lax.broadcasted_iota(jnp.int32, (8, 8), 1)
    lists[:, NEAR : NEAR + 1] = jnp.sum(
        jnp.where(row_col, near_count[...], 0), axis=1, keepdims=True
    )

    center = pts[:, 0:1]
    wide8 = lax.broadcasted_iota(jnp.int32, (8, nleaf * LEAF), 0)

    def parts(coords):
        scaled = (coords - center) * SCALE
        norm = jnp.sum(scaled * scaled, axis=0, keepdims=True)
        return split3(scaled), norm

    def left(coords, first):
        (one, two, three), norm = parts(coords)
        n1, n2, n3 = split3(norm + SCALE * SCALE * 0.0001)
        ends = jnp.where(wide8 < 6, 1.0, 0.0)
        ends = jnp.where(wide8 == 0, n1, jnp.where(wide8 == 1, n2, jnp.where(wide8 == 2, n3, ends)))
        for k, block in enumerate((one, one, two, two, one, three)):
            stage[8 * k : 8 * k + 3, :] = block
        stage[48:56, :] = ends
        for g in range(nleaf):
            left_feat[first + g] = jnp.transpose(stage[:, cols(g)]).astype(BF16)

    def right(coords):
        (one, two, three), norm = parts(coords)
        n1, n2, n3 = split3(norm)
        ends = jnp.where(wide8 < 3, 1.0, 0.0)
        ends = jnp.where(wide8 == 3, n1, jnp.where(wide8 == 4, n2, jnp.where(wide8 == 5, n3, ends)))
        one, two, three = -2.0 * one, -2.0 * two, -2.0 * three
        for k, block in enumerate((one, two, one, two, three, one)):
            stage[8 * k : 8 * k + 3, :] = block
        stage[48:56, :] = ends
        for g in range(nleaf):
            right_feat[g] = stage[:, cols(g)].astype(BF16)

    stage[...] = jnp.zeros(stage.shape, F32)
    right(pts[...])
    left(pts[...], nleaf)

    def tile(leaf, g, one, slope):
        square = jnp.dot(left_feat[leaf], right_feat[g], preferred_element_type=F32)
        root = square * lax.rsqrt(square)
        return (jnp.exp2(-root) * (one + slope * root)).astype(BF16)

    for g in range(nleaf):
        own_tiles[g] = tile(nleaf + g, g, 1.0, LN2)
    pl.semaphore_wait(barrier, len(everyone))

    side = both_ways(
        pts, (side_pts.at[0], side_pts.at[1]),
        (side_ss.at[0, 0], side_ss.at[0, 1]), (side_rs.at[0, 0], side_rs.at[0, 1]),
    ) + both_ways(
        lists, (side_lists.at[0], side_lists.at[1]),
        (side_ss.at[1, 0], side_ss.at[1, 1]), (side_rs.at[1, 0], side_rs.at[1, 1]),
    )
    values = both_ways(
        pool0.at[nleaf : 2 * nleaf], (pool0.at[0:nleaf], pool0.at[2 * nleaf :]),
        (side_ss.at[2, 0], side_ss.at[2, 1]), (side_rs.at[2, 0], side_rs.at[2, 1]),
    )
    sib = start_sib(0, coef_r0, none)
    z, mixed, total, scalars = start_z(0, sib, coef_r0, none)
    for copy in side:
        copy.wait()
    left(side_pts[0], 0)
    left(side_pts[1], 2 * nleaf)

    mine = lists[...]
    counts = mine[:, NEAR : NEAR + 1]
    place = jnp.bitwise_and(jnp.right_shift(mine, 3) - me + 1, ndev - 1)
    index = jnp.clip(place * nleaf + jnp.bitwise_and(mine, nleaf - 1), 0, 3 * nleaf - 1)
    table_v[0] = index
    table_v[2] = (slot < counts).astype(jnp.int32)
    named = jnp.zeros((8, 128), jnp.int32)
    named_active = jnp.zeros((8, 128), jnp.int32)
    for k, theirs in enumerate((side_lists[0], mine, side_lists[1])):
        live = (slot < theirs[:, NEAR : NEAR + 1]).astype(jnp.int32)
        for g in range(nleaf):
            match = theirs == me * nleaf + g
            where = jnp.sum(jnp.where(match, row8 + k * nleaf, 0), axis=0, keepdims=True)
            alive = jnp.sum(jnp.where(match, live, 0), axis=0, keepdims=True)
            named = named + jnp.where(row8 == g, where, 0)
            named_active = named_active + jnp.where(row8 == g, alive, 0)
    table_v[1] = jnp.clip(named, 0, 3 * nleaf - 1)
    table_v[3] = named_active
    times = counts + jnp.sum(jnp.where(slot < NEAR, named_active, 0), axis=1, keepdims=True)
    table_v[4] = jnp.broadcast_to(times, (8, 128))
    to_table = pltpu.make_async_copy(table_v, table, table_sem)
    to_table.start()
    to_table.wait()

    def tile_rows(k):
        return slice(k * LEAF, (k + 1) * LEAF)

    def make_tiles(g):
        for h in range(2):
            for k in range(NEAR):
                one = table[2 + h, g, k].astype(F32)
                tiles[2 * g + h, tile_rows(k), :] = tile(table[h, g, k], g, one, one * LN2)

    def near_leaf(step, g):
        for k in range(NEAR):
            gathered[:, tile_rows(k)] = pool[step][table[0, g, k]]
            gathered[:, tile_rows(NEAR + k)] = pool[step][table[1, g, k]]
        total = jnp.dot(pool[step][nleaf + g], own_tiles[g], preferred_element_type=F32)
        total = table[4, g, 0].astype(F32) * total
        for h in range(2):
            total = total + jnp.dot(
                gathered[:, h * NEAR * LEAF : (h + 1) * NEAR * LEAF], tiles[2 * g + h],
                preferred_element_type=F32,
            )
        near[g] = total
        if step < 2:
            part_src[step][g] = (scale * total).astype(BF16)
        stack(pl.ds(pl.multiple_of(g * LEAF, LEAF), LEAF), total)

    def make_both(g, carry):
        near_leaf(0, g - 1)
        make_tiles(g)
        start_part(0, g - 1)
        return carry

    make_tiles(0)
    for copy in values:
        copy.wait()
    bases = both_ways(
        basis2.at[0:64], (side_basis.at[0], side_basis.at[1]),
        (basis_ss.at[0], basis_ss.at[1]), (basis_rs.at[0], basis_rs.at[1]),
    )
    lax.fori_loop(1, 2, make_both, 0)
    xy, mixed, total, scalars = start_xy(0, z, mixed, total, scalars)
    lax.fori_loop(2, nleaf, make_both, 0)
    near_leaf(0, nleaf - 1)
    start_part(0, nleaf - 1)

    def later_near(step):
        def one_leaf(g, carry):
            near_leaf(step, g)
            if step < 2:
                start_part(step, g)
            return carry

        lax.fori_loop(0, nleaf, one_leaf, 0)

    near_coef = coeffs()
    rb = jnp.zeros((64, 128), F32)
    for g in range(nleaf):
        rb = rb + fold(rhs[:, cols(g)] * near[g])
    near_rb = scale * lanes(rb)
    packed, _ = finish(0, xy, mixed, total, scalars)
    side_coefs = send_coef(0, packed)
    both = unpack(packed)
    wide, low = widen(both)
    coef_b0 = scale * near_coef + through_gram(wide, low)
    scalars = to_row(rr_local, near_rb + lanes(unpack(coef_r0) * both))
    coef = coef_b0
    sib = start_sib(1, coef, scalars)
    for g in range(nleaf):
        value = scale * near[g] + far(g, wide, low)
        b0[:, cols(g)] = value
        put_pool(1, g, value)
    z, mixed, total, scalars = start_z(1, sib, coef, scalars)
    for copy in bases:
        copy.wait()
    side_images(0, side_coefs, lambda leaf, value: value)
    xy, mixed, total, scalars = start_xy(1, z, mixed, total, scalars)
    later_near(1)
    near_coef = coeffs()

    packed, scalars = finish(1, xy, mixed, total, scalars)
    side_coefs = send_coef(1, packed)
    both = unpack(packed)
    wide, low = widen(both)
    rr0, rb0 = from_row(scalars)
    alpha0 = rr0 / (rr0 + rb0)
    coef_y1 = scale * near_coef + through_gram(wide, low)
    coef_r1 = coef_r0 - pack(alpha0) * (coef_r0 + coef_b0)
    coef_b1 = coef_b0 - pack(alpha0) * (coef_b0 + coef_y1)
    rr = jnp.zeros((64, 128), F32)
    rb = jnp.zeros((64, 128), F32)
    for g in range(nleaf):
        one = b0[:, cols(g)]
        held = rhs[:, cols(g)]
        res = held - alpha0 * (held + one)
        r1[:, cols(g)] = res
        nxt = one - alpha0 * (one + scale * near[g])
        b1[:, cols(g)] = nxt
        rr = rr + fold(res * res)
        rb = rb + fold(res * nxt)
    scalars = to_row(lanes(rr), lanes(rb) - alpha0 * lanes(unpack(coef_r1) * both))
    coef = coef_b1
    sib = start_sib(2, coef, scalars)
    for g in range(nleaf):
        part = far(g, wide, low)
        y1[:, cols(g)] = scale * near[g] + part
        nxt = b1[:, cols(g)] - alpha0 * part
        b1[:, cols(g)] = nxt
        put_pool(2, g, nxt)
    z, mixed, total, scalars = start_z(2, sib, coef, scalars)
    side_images(
        1, side_coefs,
        lambda leaf, value: pool1[leaf].astype(F32) * (1.0 - alpha0) - alpha0 * value,
    )
    xy, mixed, total, scalars = start_xy(2, z, mixed, total, scalars)
    later_near(2)

    packed, scalars = finish(2, xy, mixed, total, scalars)
    both = unpack(packed)
    wide, low = widen(both)
    rr1, rb1 = from_row(scalars)
    beta0 = rr1 / rr0
    alpha1 = rr1 / (rr1 + rb1 - beta0 * rr1 / alpha0)
    coef_p1 = coef_r1 + pack(beta0) * coef_r0
    coef_r2 = coef_r1 - pack(alpha1) * (coef_p1 + coef_b1 + pack(beta0) * coef_b0)
    rr = jnp.zeros((64, 128), F32)
    rb = jnp.zeros((64, 128), F32)
    for g in range(nleaf):
        direction = r1[:, cols(g)] + beta0 * rhs[:, cols(g)]
        moved = b1[:, cols(g)] + beta0 * b0[:, cols(g)]
        res = r1[:, cols(g)] - alpha1 * (direction + moved)
        nxt = b1[:, cols(g)] - alpha1 * (moved + scale * near[g] + beta0 * y1[:, cols(g)])
        r2[:, cols(g)] = res
        b2[:, cols(g)] = nxt
        rr = rr + fold(res * res)
        rb = rb + fold(res * nxt)
    scalars = to_row(lanes(rr), lanes(rb) - alpha1 * lanes(unpack(coef_r2) * both))

    last_src[0] = jnp.broadcast_to(scalars, (8, 128))
    copy = send(last_src.at[0, 0:1], last_sib.at[0:1], sib_ss.at[3], sib_rs.at[3], peer(1))
    copy.wait()
    scalars = scalars + last_sib[0:1]
    for stage_num, (masks, buffer, ss, rs) in enumerate(
        ((Z_MASKS, last_z, z_ss, z_rs), (XY_MASKS, last_xy, xy_ss, xy_rs))
    ):
        last_src[1 + stage_num] = jnp.broadcast_to(scalars, (8, 128))
        copies = [
            send(last_src.at[1 + stage_num, 0:1], buffer.at[k, 0:1], ss.at[3, k], rs.at[3, k], peer(m))
            for k, m in enumerate(masks)
        ]
        if stage_num == 0:
            for g in range(nleaf):
                direction = r1[:, cols(g)] + beta0 * rhs[:, cols(g)]
                moved = b1[:, cols(g)] + beta0 * b0[:, cols(g)]
                b2[:, cols(g)] = b2[:, cols(g)] - alpha1 * far(g, wide, low)
                y1[:, cols(g)] = direction
                b0[:, cols(g)] = moved
                r1[:, cols(g)] = alpha0 * rhs[:, cols(g)] + alpha1 * direction
        for copy in copies:
            copy.wait()
        for k in range(len(masks)):
            scalars = scalars + buffer[k, 0:1]
    rr2, rb2 = from_row(scalars)
    beta1 = rr2 / rr1
    alpha2 = rr2 / (rr2 + rb2 - beta1 * rr2 / alpha1)
    for g in range(nleaf):
        direction = r2[:, cols(g)] + beta1 * y1[:, cols(g)]
        moved = b2[:, cols(g)] + beta1 * b0[:, cols(g)]
        r_out[:, cols(g)] = r2[:, cols(g)] - alpha2 * (direction + moved)
        x_out[:, cols(g)] = r1[:, cols(g)] + alpha2 * direction


def place(x_in, r_in, x_out, r_out, sems):
    first = pltpu.make_async_copy(x_in, x_out, sems.at[0])
    second = pltpu.make_async_copy(r_in, r_out, sems.at[1])
    first.start()
    second.start()
    first.wait()
    second.wait()


def body(rhs, points, basis, decay, near_list, near_count):
    nrows, npts = rhs.shape
    nleaf = npts // LEAF
    vmem = pl.BlockSpec(memory_space=pltpu.VMEM)
    field = pltpu.VMEM((nrows, npts), F32)
    dma = pltpu.SemaphoreType.DMA
    shape = jax.ShapeDtypeStruct((nrows, npts), F32)
    outs = pl.pallas_call(
        kernel,
        out_shape=(shape, shape),
        in_specs=[vmem] * 6,
        out_specs=(vmem, vmem),
        scratch_shapes=[
            pltpu.VMEM((2 * nleaf, NEAR * LEAF, LEAF), BF16),
            pltpu.VMEM((nleaf, LEAF, LEAF), BF16),
            pltpu.VMEM((3 * nleaf, LEAF, 64), BF16),
            pltpu.VMEM((nleaf, 64, LEAF), BF16),
            pltpu.VMEM((64, npts), F32),
            pltpu.VMEM((nrows, 2 * NEAR * LEAF), BF16),
            *[pltpu.VMEM((3 * nleaf, nrows, LEAF), BF16)] * 3,
            pltpu.VMEM((nleaf, nrows, LEAF), F32),
            pltpu.VMEM((256, npts), BF16),
            pltpu.VMEM((128, npts), BF16),
            pltpu.VMEM((256, 128), BF16),
            field, field, field, field, field, field,
            pltpu.VMEM((8, 128), jnp.int32),
            pltpu.VMEM((2, 3, npts), F32),
            pltpu.VMEM((2, 8, 128), jnp.int32),
            pltpu.VMEM((5, 8, 128), jnp.int32),
            pltpu.SMEM((5, 8, 128), jnp.int32),
            *[pltpu.VMEM((nleaf, nrows, LEAF), BF16)] * 2,
            *[pltpu.VMEM((2, nleaf, nrows, LEAF), BF16)] * 2,
            pltpu.VMEM((2, 64, npts), BF16),
            pltpu.VMEM((2, 32, 128), BF16),
            pltpu.VMEM((2, 2, 32, 128), BF16),
            pltpu.VMEM((9, 48, 128), BF16),
            pltpu.VMEM((3, 48, 128), BF16),
            pltpu.VMEM((3, N_Z, 48, 128), BF16),
            pltpu.VMEM((3, N_XY, 48, 128), BF16),
            pltpu.VMEM((3, 8, 128), F32),
            pltpu.VMEM((8, 128), F32),
            pltpu.VMEM((N_Z, 8, 128), F32),
            pltpu.VMEM((N_XY, 8, 128), F32),
            dma((3, 2)), dma((3, 2)), dma((4,)), dma((4,)),
            dma((4, N_Z)), dma((4, N_Z)), dma((4, N_XY)), dma((4, N_XY)),
            dma((2, 2)), dma((2, 2)),
            dma((2,)), dma((2,)), dma((2, 2)), dma((2, 2)),
            dma,
        ],
        compiler_params=pltpu.CompilerParams(
            collective_id=0, has_side_effects=True, vmem_limit_bytes=56 * 2**20
        ),
    )(rhs, points, basis, decay[None, :], near_list, near_count[None, :])
    anywhere = pl.BlockSpec(memory_space=pl.ANY)
    return pl.pallas_call(
        place,
        out_shape=(shape, shape),
        in_specs=[anywhere] * 2,
        out_specs=(anywhere, anywhere),
        scratch_shapes=[dma((2,))],
    )(*outs)


def solution(mesh):
    in_specs = (
        P(None, ("leaf", "sub")),
        P(None, ("leaf", "sub")),
        P(None, ("leaf", "sub")),
        P(),
        P(("leaf", "sub"), None),
        P(("leaf", "sub")),
    )
    out_specs = (P(None, ("leaf", "sub")), P(None, ("leaf", "sub")))
    return jax.shard_map(body, mesh=mesh, in_specs=in_specs, out_specs=out_specs, check_vma=False)
```

```python
import math
import jax
import jax.numpy as jnp
from jax import lax
from jax.experimental import pallas as pl
from jax.experimental.pallas import tpu as pltpu
from jax.sharding import PartitionSpec as P

LEAF = 256
NEAR = 8
MESH = pl.DeviceIdType.MESH
F32 = jnp.float32
BF16 = jnp.bfloat16
SCALE = math.sqrt(3.0) / 0.08 * math.log2(math.e)
LN2 = math.log(2.0)
RING_HOPS = (0, 1, 2, 1)
Z_MASKS = (8, 10, 6, 12, 14, 4, 2)
XY_MASKS = tuple(
    sorted(range(16, 256, 16), key=lambda m: -(RING_HOPS[(m >> 4) & 3] + RING_HOPS[m >> 6]))
)
N_Z = len(Z_MASKS)
N_XY = len(XY_MASKS)


def level_of(mask):
    return mask.bit_length()


def split2(value):
    high = value.astype(BF16)
    return high, (value - high.astype(F32)).astype(BF16)


def split3(value):
    high = value.astype(BF16).astype(F32)
    rest = value - high
    mid = rest.astype(BF16).astype(F32)
    low = (rest - mid).astype(BF16).astype(F32)
    return high, mid, low


def kernel(
    rhs, pts, basis, decay, near_list, near_count, x_out, r_out,
    tiles, own_tiles, left_feat, right_feat, stage, gathered, pool0, pool1, pool2, near,
    basis2, stacked, gram, b0, y1, r1, b1, r2, b2, lists, side_pts, side_lists, table_v, table,
    part_src0, part_src1, part_in0, part_in1, side_basis, coef_src, coef_in,
    src, sib_in, z_in, xy_in, last_src, last_sib, last_z, last_xy,
    side_ss, side_rs, sib_ss, sib_rs, z_ss, z_rs, xy_ss, xy_rs, part_ss, part_rs,
    basis_ss, basis_rs, coef_ss, coef_rs, table_sem,
):
    nleaf = rhs.shape[1] // LEAF
    pool = (pool0, pool1, pool2)
    part_src = (part_src0, part_src1)
    part_in = (part_in0, part_in1)
    scale = 2.0 / LEAF
    me = lax.axis_index("leaf") * 2 + lax.axis_index("sub")
    ndev = 256

    def at(index):
        return (index // 2, lax.rem(index, 2))

    def peer(mask):
        return at(jnp.bitwise_xor(me, mask))

    prev, following = lax.rem(me + ndev - 1, ndev), lax.rem(me + 1, ndev)
    barrier = pltpu.get_barrier_semaphore()
    everyone = [peer(m) for m in Z_MASKS + XY_MASKS] + [at(prev), at(following), peer(1)]
    for other in everyone:
        pl.semaphore_signal(barrier, inc=1, device_id=other, device_id_type=MESH)

    def send(source, target, send_sem, recv_sem, device):
        copy = pltpu.make_async_remote_copy(
            src_ref=source, dst_ref=target, send_sem=send_sem, recv_sem=recv_sem,
            device_id=device, device_id_type=MESH,
        )
        copy.start()
        return copy

    def cols(g):
        return slice(g * LEAF, (g + 1) * LEAF)

    def put_pool(step, g, value):
        pool[step][nleaf + g] = value.astype(BF16)

    def both_ways(source, targets, send_sems, recv_sems):
        return [
            send(source, targets[0], send_sems[0], recv_sems[0], at(following)),
            send(source, targets[1], send_sems[1], recv_sems[1], at(prev)),
        ]

    def part_copies(step, leaves):
        return [
            pltpu.make_async_remote_copy(
                src_ref=part_src[step].at[leaves], dst_ref=part_in[step].at[side, leaves],
                send_sem=part_ss.at[step, side], recv_sem=part_rs.at[step, side],
                device_id=device, device_id_type=MESH,
            )
            for side, device in enumerate((at(following), at(prev)))
        ]

    def start_part(step, g):
        for copy in part_copies(step, g):
            copy.start()

    def send_coef(step, packed):
        coef_src[step] = packed.astype(BF16)
        return both_ways(
            coef_src.at[step], (coef_in.at[step, 0], coef_in.at[step, 1]),
            (coef_ss.at[step, 0], coef_ss.at[step, 1]), (coef_rs.at[step, 0], coef_rs.at[step, 1]),
        )

    def side_images(step, copies, combine):
        for copy in copies:
            copy.wait()
        for copy in part_copies(step, slice(0, nleaf)):
            copy.wait()
        for side in range(2):
            packed = coef_in[step, side].astype(F32)
            turned = pltpu.roll(packed, 64, 1)
            narrow = jnp.concatenate([packed[:, 0:64], turned[:, 0:64]], axis=0).astype(BF16)
            for g in range(nleaf):
                part = jnp.dot(narrow, side_basis[side, :, cols(g)], preferred_element_type=F32)
                leaf = 2 * nleaf * side + g
                value = part_in[step][side, g].astype(F32) + part
                pool[step + 1][leaf] = combine(leaf, value).astype(BF16)

    lane = lax.broadcasted_iota(jnp.int32, (32, 128), 1)
    low_half = lane < 64
    row16 = lax.broadcasted_iota(jnp.int32, (16, 128), 0)
    row64 = lax.broadcasted_iota(jnp.int32, (64, 128), 0)
    col64 = lax.broadcasted_iota(jnp.int32, (64, 128), 1)

    def to_row(first, second):
        spread = jnp.where(col64 == row64, first, 0.0) + jnp.where(col64 == row64 + 64, second, 0.0)
        return jnp.sum(spread, axis=0, keepdims=True)

    def from_row(row):
        first = jnp.sum(jnp.where(col64 == row64, row, 0.0), axis=1, keepdims=True)
        second = jnp.sum(jnp.where(col64 == row64 + 64, row, 0.0), axis=1, keepdims=True)
        return first, second

    def fold(value):
        return value[:, 0:128] + value[:, 128:256]

    def lanes(value):
        return jnp.sum(value, axis=1, keepdims=True)

    def pack(value):
        value = jnp.broadcast_to(value, (64, 128))
        return jnp.where(low_half, value[0:32], value[32:64])

    def unpack(value):
        return jnp.concatenate(
            [jnp.where(low_half, value, 0.0), jnp.where(low_half, 0.0, value)], axis=0
        )

    decay2 = jnp.concatenate([decay[...], decay[...]], axis=1)
    weights = [None, decay2]
    for _ in range(7):
        weights.append(weights[-1] * decay2 * math.sqrt(0.5))

    def stack(where, value):
        high, low = split2(value)
        stacked[0:64, where] = high
        stacked[64:128, where] = low

    def coeffs():
        full = lax.dot_general(
            stacked[...], basis2[...], (((1,), (1,)), ((), ())), preferred_element_type=F32
        )
        return pack(full[0:64, 0:128] + full[64:128, 0:128] + full[0:64, 128:256])

    def write_message(slot, coef, scalars):
        high, mid, low = split3(scalars)
        rows = jnp.where(row16 == 0, high, jnp.where(row16 == 1, mid, jnp.where(row16 == 2, low, 0.0)))
        src[slot, 0:32] = coef.astype(BF16)
        src[slot, 32:48] = rows.astype(BF16)

    def read_message(ref):
        return ref[0:32].astype(F32), jnp.sum(ref[32:48].astype(F32), axis=0, keepdims=True)

    def start_sib(step, coef, scalars):
        write_message(3 * step, coef, scalars)
        return send(src.at[3 * step], sib_in.at[step], sib_ss.at[step], sib_rs.at[step], peer(1))

    def start_z(step, copy, coef, scalars):
        copy.wait()
        other, other_scalars = read_message(sib_in.at[step])
        mixed = coef + weights[1] * other
        total, scalars = coef + other, scalars + other_scalars
        write_message(3 * step + 1, total, scalars)
        copies = [
            send(src.at[3 * step + 1], z_in.at[step, k], z_ss.at[step, k], z_rs.at[step, k], peer(m))
            for k, m in enumerate(Z_MASKS)
        ]
        return copies, mixed, total, scalars

    def collect(copies, masks, buffer, mixed, total, scalars):
        for copy in copies:
            copy.wait()
        levels = {}
        for k, mask in enumerate(masks):
            other, other_scalars = read_message(buffer.at[k])
            level = level_of(mask)
            levels[level] = other if level not in levels else levels[level] + other
            scalars = scalars + other_scalars
        for level, other in levels.items():
            mixed = mixed + weights[level] * other
            total = total + other
        return mixed, total, scalars

    def start_xy(step, copies, mixed, total, scalars):
        mixed, total, scalars = collect(copies, Z_MASKS, z_in.at[step], mixed, total, scalars)
        write_message(3 * step + 2, total, scalars)
        copies = [
            send(src.at[3 * step + 2], xy_in.at[step, k], xy_ss.at[step, k], xy_rs.at[step, k], peer(m))
            for k, m in enumerate(XY_MASKS)
        ]
        return copies, mixed, total, scalars

    def finish(step, copies, mixed, total, scalars):
        mixed, _, scalars = collect(copies, XY_MASKS, xy_in.at[step], mixed, total, scalars)
        return mixed, scalars

    def widen(both):
        high, low = split2(both)
        return jnp.concatenate([high, high], axis=1), low

    def far(g, wide, low):
        part = jnp.dot(wide, basis2[:, cols(g)], preferred_element_type=F32)
        return part + jnp.dot(low, basis2[0:128, cols(g)], preferred_element_type=F32)

    def through_gram(wide, low):
        part = jnp.dot(wide, gram[...], preferred_element_type=F32)
        return pack(part + jnp.dot(low, gram[0:128], preferred_element_type=F32))

    high, low = split2(basis[...])
    basis2[0:64] = high
    basis2[64:128] = high
    basis2[128:192] = low
    basis2[192:256] = low
    rr = jnp.zeros((64, 128), F32)
    for g in range(nleaf):
        held = rhs[:, cols(g)]
        put_pool(0, g, held)
        stack(cols(g), held)
        rr = rr + fold(held * held)
    rr_local = lanes(rr)
    coef_r0 = coeffs()
    none = jnp.zeros((1, 128), F32)
    full = lax.dot_general(
        basis2[...], basis2[...], (((1,), (1,)), ((), ())), preferred_element_type=F32
    )
    full = full[0:128, 0:128] + full[0:128, 128:256] + full[128:256, 0:128]
    gram[0:128], gram[128:256] = split2(full)
    row8 = lax.broadcasted_iota(jnp.int32, (8, 128), 0)
    slot = lax.broadcasted_iota(jnp.int32, (8, 128), 1)
    lists[...] = jnp.zeros((8, 128), jnp.int32)
    lists[:, 0:NEAR] = near_list[...]
    row_col = lax.broadcasted_iota(jnp.int32, (8, 8), 0) == lax.broadcasted_iota(jnp.int32, (8, 8), 1)
    lists[:, NEAR : NEAR + 1] = jnp.sum(
        jnp.where(row_col, near_count[...], 0), axis=1, keepdims=True
    )

    center = pts[:, 0:1]
    wide8 = lax.broadcasted_iota(jnp.int32, (8, nleaf * LEAF), 0)

    def parts(coords):
        scaled = (coords - center) * SCALE
        norm = jnp.sum(scaled * scaled, axis=0, keepdims=True)
        return split3(scaled), norm

    def left(coords, first):
        (one, two, three), norm = parts(coords)
        n1, n2, n3 = split3(norm + SCALE * SCALE * 0.0001)
        ends = jnp.where(wide8 < 6, 1.0, 0.0)
        ends = jnp.where(wide8 == 0, n1, jnp.where(wide8 == 1, n2, jnp.where(wide8 == 2, n3, ends)))
        for k, block in enumerate((one, one, two, two, one, three)):
            stage[8 * k : 8 * k + 3, :] = block
        stage[48:56, :] = ends
        for g in range(nleaf):
            left_feat[first + g] = jnp.transpose(stage[:, cols(g)]).astype(BF16)

    def right(coords):
        (one, two, three), norm = parts(coords)
        n1, n2, n3 = split3(norm)
        ends = jnp.where(wide8 < 3, 1.0, 0.0)
        ends = jnp.where(wide8 == 3, n1, jnp.where(wide8 == 4, n2, jnp.where(wide8 == 5, n3, ends)))
        one, two, three = -2.0 * one, -2.0 * two, -2.0 * three
        for k, block in enumerate((one, two, one, two, three, one)):
            stage[8 * k : 8 * k + 3, :] = block
        stage[48:56, :] = ends
        for g in range(nleaf):
            right_feat[g] = stage[:, cols(g)].astype(BF16)

    stage[...] = jnp.zeros(stage.shape, F32)
    right(pts[...])
    left(pts[...], nleaf)

    def tile(leaf, g, one, slope):
        square = jnp.dot(left_feat[leaf], right_feat[g], preferred_element_type=F32)
        root = square * lax.rsqrt(square)
        return (jnp.exp2(-root) * (one + slope * root)).astype(BF16)

    for g in range(nleaf):
        own_tiles[g] = tile(nleaf + g, g, 1.0, LN2)
    pl.semaphore_wait(barrier, len(everyone))

    side = both_ways(
        pts, (side_pts.at[0], side_pts.at[1]),
        (side_ss.at[0, 0], side_ss.at[0, 1]), (side_rs.at[0, 0], side_rs.at[0, 1]),
    ) + both_ways(
        lists, (side_lists.at[0], side_lists.at[1]),
        (side_ss.at[1, 0], side_ss.at[1, 1]), (side_rs.at[1, 0], side_rs.at[1, 1]),
    )
    values = both_ways(
        pool0.at[nleaf : 2 * nleaf], (pool0.at[0:nleaf], pool0.at[2 * nleaf :]),
        (side_ss.at[2, 0], side_ss.at[2, 1]), (side_rs.at[2, 0], side_rs.at[2, 1]),
    )
    sib = start_sib(0, coef_r0, none)
    z, mixed, total, scalars = start_z(0, sib, coef_r0, none)
    for copy in side:
        copy.wait()
    left(side_pts[0], 0)
    left(side_pts[1], 2 * nleaf)

    mine = lists[...]
    counts = mine[:, NEAR : NEAR + 1]
    place = jnp.bitwise_and(jnp.right_shift(mine, 3) - me + 1, ndev - 1)
    index = jnp.clip(place * nleaf + jnp.bitwise_and(mine, nleaf - 1), 0, 3 * nleaf - 1)
    table_v[0] = index
    table_v[2] = (slot < counts).astype(jnp.int32)
    named = jnp.zeros((8, 128), jnp.int32)
    named_active = jnp.zeros((8, 128), jnp.int32)
    for k, theirs in enumerate((side_lists[0], mine, side_lists[1])):
        live = (slot < theirs[:, NEAR : NEAR + 1]).astype(jnp.int32)
        for g in range(nleaf):
            match = theirs == me * nleaf + g
            where = jnp.sum(jnp.where(match, row8 + k * nleaf, 0), axis=0, keepdims=True)
            alive = jnp.sum(jnp.where(match, live, 0), axis=0, keepdims=True)
            named = named + jnp.where(row8 == g, where, 0)
            named_active = named_active + jnp.where(row8 == g, alive, 0)
    table_v[1] = jnp.clip(named, 0, 3 * nleaf - 1)
    table_v[3] = named_active
    times = counts + jnp.sum(jnp.where(slot < NEAR, named_active, 0), axis=1, keepdims=True)
    table_v[4] = jnp.broadcast_to(times, (8, 128))
    to_table = pltpu.make_async_copy(table_v, table, table_sem)
    to_table.start()
    to_table.wait()

    def tile_rows(k):
        return slice(k * LEAF, (k + 1) * LEAF)

    def make_tiles(g):
        for h in range(2):
            for k in range(NEAR):
                one = table[2 + h, g, k].astype(F32)
                tiles[2 * g + h, tile_rows(k), :] = tile(table[h, g, k], g, one, one * LN2)

    def near_leaf(step, g):
        for k in range(NEAR):
            gathered[:, tile_rows(k)] = pool[step][table[0, g, k]]
            gathered[:, tile_rows(NEAR + k)] = pool[step][table[1, g, k]]
        total = jnp.dot(pool[step][nleaf + g], own_tiles[g], preferred_element_type=F32)
        total = table[4, g, 0].astype(F32) * total
        for h in range(2):
            total = total + jnp.dot(
                gathered[:, h * NEAR * LEAF : (h + 1) * NEAR * LEAF], tiles[2 * g + h],
                preferred_element_type=F32,
            )
        near[g] = total
        if step < 2:
            part_src[step][g] = (scale * total).astype(BF16)
        stack(pl.ds(pl.multiple_of(g * LEAF, LEAF), LEAF), total)

    def make_both(g, carry):
        near_leaf(0, g - 1)
        make_tiles(g)
        start_part(0, g - 1)
        return carry

    make_tiles(0)
    for copy in values:
        copy.wait()
    bases = both_ways(
        basis2.at[0:64], (side_basis.at[0], side_basis.at[1]),
        (basis_ss.at[0], basis_ss.at[1]), (basis_rs.at[0], basis_rs.at[1]),
    )
    lax.fori_loop(1, 2, make_both, 0)
    xy, mixed, total, scalars = start_xy(0, z, mixed, total, scalars)
    lax.fori_loop(2, nleaf, make_both, 0)
    near_leaf(0, nleaf - 1)
    start_part(0, nleaf - 1)

    def later_near(step):
        def one_leaf(g, carry):
            near_leaf(step, g)
            if step < 2:
                start_part(step, g)
            return carry

        lax.fori_loop(0, nleaf, one_leaf, 0)

    near_coef = coeffs()
    rb = jnp.zeros((64, 128), F32)
    for g in range(nleaf):
        rb = rb + fold(rhs[:, cols(g)] * near[g])
    near_rb = scale * lanes(rb)
    packed, _ = finish(0, xy, mixed, total, scalars)
    side_coefs = send_coef(0, packed)
    both = unpack(packed)
    wide, low = widen(both)
    coef_b0 = scale * near_coef + through_gram(wide, low)
    scalars = to_row(rr_local, near_rb + lanes(unpack(coef_r0) * both))
    coef = coef_b0
    sib = start_sib(1, coef, scalars)
    for g in range(nleaf):
        value = scale * near[g] + far(g, wide, low)
        b0[:, cols(g)] = value
        put_pool(1, g, value)
    z, mixed, total, scalars = start_z(1, sib, coef, scalars)
    for copy in bases:
        copy.wait()
    side_images(0, side_coefs, lambda leaf, value: value)
    xy, mixed, total, scalars = start_xy(1, z, mixed, total, scalars)
    later_near(1)
    near_coef = coeffs()

    packed, scalars = finish(1, xy, mixed, total, scalars)
    side_coefs = send_coef(1, packed)
    both = unpack(packed)
    wide, low = widen(both)
    rr0, rb0 = from_row(scalars)
    alpha0 = rr0 / (rr0 + rb0)
    coef_y1 = scale * near_coef + through_gram(wide, low)
    coef_r1 = coef_r0 - pack(alpha0) * (coef_r0 + coef_b0)
    coef_b1 = coef_b0 - pack(alpha0) * (coef_b0 + coef_y1)
    rr = jnp.zeros((64, 128), F32)
    rb = jnp.zeros((64, 128), F32)
    for g in range(nleaf):
        one = b0[:, cols(g)]
        held = rhs[:, cols(g)]
        res = held - alpha0 * (held + one)
        r1[:, cols(g)] = res
        nxt = one - alpha0 * (one + scale * near[g])
        b1[:, cols(g)] = nxt
        rr = rr + fold(res * res)
        rb = rb + fold(res * nxt)
    scalars = to_row(lanes(rr), lanes(rb) - alpha0 * lanes(unpack(coef_r1) * both))
    coef = coef_b1
    sib = start_sib(2, coef, scalars)
    for g in range(nleaf):
        part = far(g, wide, low)
        y1[:, cols(g)] = scale * near[g] + part
        nxt = b1[:, cols(g)] - alpha0 * part
        b1[:, cols(g)] = nxt
        put_pool(2, g, nxt)
    z, mixed, total, scalars = start_z(2, sib, coef, scalars)
    side_images(
        1, side_coefs,
        lambda leaf, value: pool1[leaf].astype(F32) * (1.0 - alpha0) - alpha0 * value,
    )
    xy, mixed, total, scalars = start_xy(2, z, mixed, total, scalars)
    later_near(2)

    packed, scalars = finish(2, xy, mixed, total, scalars)
    both = unpack(packed)
    wide, low = widen(both)
    rr1, rb1 = from_row(scalars)
    beta0 = rr1 / rr0
    alpha1 = rr1 / (rr1 + rb1 - beta0 * rr1 / alpha0)
    coef_p1 = coef_r1 + pack(beta0) * coef_r0
    coef_r2 = coef_r1 - pack(alpha1) * (coef_p1 + coef_b1 + pack(beta0) * coef_b0)
    rr = jnp.zeros((64, 128), F32)
    rb = jnp.zeros((64, 128), F32)
    for g in range(nleaf):
        direction = r1[:, cols(g)] + beta0 * rhs[:, cols(g)]
        moved = b1[:, cols(g)] + beta0 * b0[:, cols(g)]
        res = r1[:, cols(g)] - alpha1 * (direction + moved)
        nxt = b1[:, cols(g)] - alpha1 * (moved + scale * near[g] + beta0 * y1[:, cols(g)])
        r2[:, cols(g)] = res
        b2[:, cols(g)] = nxt
        rr = rr + fold(res * res)
        rb = rb + fold(res * nxt)
    scalars = to_row(lanes(rr), lanes(rb) - alpha1 * lanes(unpack(coef_r2) * both))

    last_src[0] = jnp.broadcast_to(scalars, (8, 128))
    copy = send(last_src.at[0, 0:1], last_sib.at[0:1], sib_ss.at[3], sib_rs.at[3], peer(1))
    copy.wait()
    scalars = scalars + last_sib[0:1]
    for stage_num, (masks, buffer, ss, rs) in enumerate(
        ((Z_MASKS, last_z, z_ss, z_rs), (XY_MASKS, last_xy, xy_ss, xy_rs))
    ):
        last_src[1 + stage_num] = jnp.broadcast_to(scalars, (8, 128))
        copies = [
            send(last_src.at[1 + stage_num, 0:1], buffer.at[k, 0:1], ss.at[3, k], rs.at[3, k], peer(m))
            for k, m in enumerate(masks)
        ]
        if stage_num == 0:
            for g in range(nleaf):
                direction = r1[:, cols(g)] + beta0 * rhs[:, cols(g)]
                moved = b1[:, cols(g)] + beta0 * b0[:, cols(g)]
                b2[:, cols(g)] = b2[:, cols(g)] - alpha1 * far(g, wide, low)
                y1[:, cols(g)] = direction
                b0[:, cols(g)] = moved
                r1[:, cols(g)] = alpha0 * rhs[:, cols(g)] + alpha1 * direction
        for copy in copies:
            copy.wait()
        for k in range(len(masks)):
            scalars = scalars + buffer[k, 0:1]
    rr2, rb2 = from_row(scalars)
    beta1 = rr2 / rr1
    alpha2 = rr2 / (rr2 + rb2 - beta1 * rr2 / alpha1)
    for g in range(nleaf):
        direction = r2[:, cols(g)] + beta1 * y1[:, cols(g)]
        moved = b2[:, cols(g)] + beta1 * b0[:, cols(g)]
        r_out[:, cols(g)] = r2[:, cols(g)] - alpha2 * (direction + moved)
        x_out[:, cols(g)] = r1[:, cols(g)] + alpha2 * direction


def place(x_in, r_in, x_out, r_out, hold, sems):
    reads = [
        pltpu.make_async_copy(source, hold.at[k], sems.at[k])
        for k, source in enumerate((x_in, r_in))
    ]
    for copy in reads:
        copy.start()
    writes = [
        pltpu.make_async_copy(hold.at[k], target, sems.at[2 + k])
        for k, target in enumerate((x_out, r_out))
    ]
    for read, write in zip(reads, writes):
        read.wait()
        write.start()
    for copy in writes:
        copy.wait()


def body(rhs, points, basis, decay, near_list, near_count):
    nrows, npts = rhs.shape
    nleaf = npts // LEAF
    vmem = pl.BlockSpec(memory_space=pltpu.VMEM)
    field = pltpu.VMEM((nrows, npts), F32)
    dma = pltpu.SemaphoreType.DMA
    shape = jax.ShapeDtypeStruct((nrows, npts), F32)
    outs = pl.pallas_call(
        kernel,
        out_shape=(shape, shape),
        in_specs=[vmem] * 6,
        out_specs=(vmem, vmem),
        scratch_shapes=[
            pltpu.VMEM((2 * nleaf, NEAR * LEAF, LEAF), BF16),
            pltpu.VMEM((nleaf, LEAF, LEAF), BF16),
            pltpu.VMEM((3 * nleaf, LEAF, 64), BF16),
            pltpu.VMEM((nleaf, 64, LEAF), BF16),
            pltpu.VMEM((64, npts), F32),
            pltpu.VMEM((nrows, 2 * NEAR * LEAF), BF16),
            *[pltpu.VMEM((3 * nleaf, nrows, LEAF), BF16)] * 3,
            pltpu.VMEM((nleaf, nrows, LEAF), F32),
            pltpu.VMEM((256, npts), BF16),
            pltpu.VMEM((128, npts), BF16),
            pltpu.VMEM((256, 128), BF16),
            field, field, field, field, field, field,
            pltpu.VMEM((8, 128), jnp.int32),
            pltpu.VMEM((2, 3, npts), F32),
            pltpu.VMEM((2, 8, 128), jnp.int32),
            pltpu.VMEM((5, 8, 128), jnp.int32),
            pltpu.SMEM((5, 8, 128), jnp.int32),
            *[pltpu.VMEM((nleaf, nrows, LEAF), BF16)] * 2,
            *[pltpu.VMEM((2, nleaf, nrows, LEAF), BF16)] * 2,
            pltpu.VMEM((2, 64, npts), BF16),
            pltpu.VMEM((2, 32, 128), BF16),
            pltpu.VMEM((2, 2, 32, 128), BF16),
            pltpu.VMEM((9, 48, 128), BF16),
            pltpu.VMEM((3, 48, 128), BF16),
            pltpu.VMEM((3, N_Z, 48, 128), BF16),
            pltpu.VMEM((3, N_XY, 48, 128), BF16),
            pltpu.VMEM((3, 8, 128), F32),
            pltpu.VMEM((8, 128), F32),
            pltpu.VMEM((N_Z, 8, 128), F32),
            pltpu.VMEM((N_XY, 8, 128), F32),
            dma((3, 2)), dma((3, 2)), dma((4,)), dma((4,)),
            dma((4, N_Z)), dma((4, N_Z)), dma((4, N_XY)), dma((4, N_XY)),
            dma((2, 2)), dma((2, 2)),
            dma((2,)), dma((2,)), dma((2, 2)), dma((2, 2)),
            dma,
        ],
        compiler_params=pltpu.CompilerParams(
            collective_id=0, has_side_effects=True, vmem_limit_bytes=56 * 2**20
        ),
    )(rhs, points, basis, decay[None, :], near_list, near_count[None, :])
    anywhere = pl.BlockSpec(memory_space=pl.ANY)
    return pl.pallas_call(
        place,
        out_shape=(shape, shape),
        in_specs=[anywhere] * 2,
        out_specs=(anywhere, anywhere),
        scratch_shapes=[pltpu.VMEM((2, nrows, npts), F32), dma((4,))],
    )(*outs)


def solution(mesh):
    in_specs = (
        P(None, ("leaf", "sub")),
        P(None, ("leaf", "sub")),
        P(None, ("leaf", "sub")),
        P(),
        P(("leaf", "sub"), None),
        P(("leaf", "sub")),
    )
    out_specs = (P(None, ("leaf", "sub")), P(None, ("leaf", "sub")))
    return jax.shard_map(body, mesh=mesh, in_specs=in_specs, out_specs=out_specs, check_vma=False)
```
